256 devices in a mesh: aux: 8 (over x, y_hi), occ: 16 (over z, core), pair: 2 (over y_lo).
Axes of the slice: x: 4, y: 4 (y_hi: 2, y_lo: 2; y = y_hi * 2 + y_lo), z: 8, core: 2. Of those that a mesh axis runs over, the one named last changes fastest.
Arguments:
- first_factors: bfloat16 [4096, 2, 4096], P(('aux', 'occ')), may hold values from -0.75 to 0.75
- second_factors: bfloat16 [4096, 32, 4096], P(('aux', 'occ', 'pair')), may hold values from -0.75 to 0.75
- first_energy: float32 [2], replicated, may hold values from -1.2 to -0.3
- second_energy: float32 [32], P(('occ', 'pair')), may hold values from -1.2 to -0.3
- virtual_energy: float32 [4096], replicated, may hold values from 0.2 to 4
- kept_blocks: int32 [2, 32, 64, 2], P(None, ('occ', 'pair')), may hold values from 0 to 63, all different within a row
Outputs:
- first_density: bfloat16 [4096, 2, 4096], P('aux', 'pair', 'occ')
- second_density: bfloat16 [4096, 32, 4096], P('aux', ('occ', 'pair'))
The draws below stay inside these ranges and needn't reach their ends.
Inputs may be any that keep to these rules, and one draw needn't show every extreme that they name: Each row kept_blocks[i, j, A, :] names 2 different blocks.
All inputs are finite; a program needn't handle non-finite values.
Results may differ from the reference program's by a relative error of at most 0.0048.
Values may be sent and summed in bfloat16 or wider, within the bound.
A program may use at most 128 MiB of HBM per device.

```python
import math
import jax
import jax.numpy as jnp
from jax import lax

NAUX = 4096
V = 4096
BLK = 64
NI = 2
NB = 64
KB = 2
NJ = 32


def shard_levels(stream_key, dims, shards, low, top_value):
    factor_of, own = 1.0, jax.random.fold_in(stream_key, 6)
    for position, shards_of in shards:
        heights = jnp.exp(jax.random.uniform(jax.random.fold_in(own, position), (shards_of,), jnp.float32, low / len(shards), top_value / len(shards)))
        factor_of = factor_of * jnp.repeat(heights, dims[position] // shards_of).reshape([-1 if axis == position else 1 for axis in range(len(dims))])
    return factor_of


def different_ones(rng, rows, count, top, lift):
    order = jax.random.permutation(jax.random.fold_in(rng, 1), count)
    boost = order
    for power in range(3):
        boost = boost * boost // count
    boost = boost * lift // count
    chance = jax.random.randint(jax.random.fold_in(rng, 2), (rows, count), 0, 4096) + boost
    fixed_rows = jax.random.permutation(jax.random.fold_in(rng, 3), rows)[jnp.arange(count) % rows]
    chance = jnp.where(jnp.arange(rows)[:, None] == fixed_rows[None, :], 1 << 14, chance)
    merit = chance * count + jnp.arange(count)
    return lax.top_k(merit.astype(jnp.int32), top)[1].astype(jnp.int32)


def gaussian(stream_key, dims, deviation, most, pieces=(), kind=jnp.bfloat16):
    loudness = shard_levels(stream_key, dims, pieces, -0.22, 0.18) if pieces else 1.0
    values = jax.random.normal(stream_key, dims, jnp.float32) * deviation * loudness
    return jnp.minimum(jnp.maximum(values, -most), most).astype(kind)


def setup_inputs(seed: int = 0) -> dict:
    arg_keys = jax.random.split(jax.random.key(seed), 7)
    first_factors = gaussian(arg_keys[0], (NAUX, NI, V), 0.125, 0.75, ((0, 128),))
    second_factors = gaussian(arg_keys[1], (NAUX, NJ, V), 0.125, 0.75, ((0, 256),))
    first_energy = jnp.clip(jax.random.uniform(arg_keys[2], (NI,), jnp.float32, -1.2, -0.3), -1.2, -0.3)
    second_energy = jnp.clip(-1.2 + 0.90000004 * jax.random.uniform(arg_keys[3], (NJ,), jnp.float32) ** shard_levels(arg_keys[3], (NJ,), ((0, 32),), -0.2, 0.2), -1.2, -0.3)
    virtual_energy = jnp.clip(jnp.exp(jax.random.uniform(arg_keys[4], (V,), jnp.float32, math.log(0.2), math.log(4.0))), 0.2, 4.0)
    kept_blocks = different_ones(arg_keys[5], NI * NJ * NB, NB, KB, 256).reshape((NI, NJ, NB, KB))
    return dict(first_factors=first_factors, second_factors=second_factors, first_energy=first_energy, second_energy=second_energy, virtual_energy=virtual_energy, kept_blocks=kept_blocks)


def reference(first_factors, second_factors, first_energy, second_energy, virtual_energy, kept_blocks):
    aux_rows = first_factors.shape[0]
    block_count = V // BLK
    kept_count = kept_blocks.shape[3]
    energy_blocks = virtual_energy.reshape(block_count, BLK)
    energy_left = jnp.repeat(energy_blocks, kept_count, axis=0)

    def per_second(first_total, index_second):
        rows_second = lax.dynamic_index_in_dim(second_factors, index_second, 1, keepdims=False)
        right_all = rows_second.reshape(aux_rows, block_count, BLK)
        energy_second = lax.dynamic_index_in_dim(second_energy, index_second, 0, keepdims=False)
        picked_all = lax.dynamic_index_in_dim(kept_blocks, index_second, 1, keepdims=False)
        second_total = jnp.zeros((aux_rows, block_count, BLK), jnp.float32)
        for index_first in range(NI):
            picked = picked_all[index_first].reshape(-1).astype(jnp.int32)
            left_rows = jnp.repeat(first_factors[:, index_first].reshape(aux_rows, block_count, BLK), kept_count, axis=1).astype(jnp.float32)
            right_rows = jnp.take(right_all, picked, axis=1).astype(jnp.float32)
            intersection = jnp.einsum("pna,pnb->nab", left_rows, right_rows)
            energy_right = jnp.take(energy_blocks, picked, axis=0)
            divisor = energy_left[:, :, None] + energy_right[:, None, :] - first_energy[index_first] - energy_second
            rounded = (intersection / divisor).astype(jnp.bfloat16)
            amplitude = lax.optimization_barrier(rounded).astype(jnp.float32)
            toward_first = jnp.einsum("nab,pnb->pna", amplitude, right_rows)
            toward_first = toward_first.reshape(aux_rows, block_count, kept_count, BLK).sum(axis=2).reshape(aux_rows, V)
            first_total = first_total.at[:, index_first].add(toward_first)
            toward_second = jnp.einsum("nab,pna->pnb", amplitude, left_rows)
            second_total = second_total.at[:, picked].add(toward_second)
        return first_total, second_total.reshape(aux_rows, V).astype(jnp.bfloat16)

    first_total, second_all = lax.scan(per_second, jnp.zeros((aux_rows, NI, V), jnp.float32), jnp.arange(NJ, dtype=jnp.int32))
    return first_total.astype(jnp.bfloat16), jnp.transpose(second_all, (1, 0, 2))
```

```python
import functools

import jax
import jax.numpy as jnp
from jax import lax
from jax.experimental import pallas as pl
from jax.experimental.pallas import tpu as pltpu
from jax.sharding import PartitionSpec as P

MESH = pl.DeviceIdType.MESH
F32 = jnp.float32
BF16 = jnp.bfloat16
BLK = 64
LANES = 128
NX = 4
VMEM_LIMIT = 52 * 1024 * 1024


def place():
    aux, occ, pair = lax.axis_index("aux"), lax.axis_index("occ"), lax.axis_index("pair")
    return aux, occ // 2, occ % 2, pair


def device(aux, z, core, pair):
    return {"aux": aux, "occ": z * 2 + core, "pair": pair}


def push(src, dst, send, recv, to):
    copy = pltpu.make_async_remote_copy(
        src_ref=src, dst_ref=dst, send_sem=send, recv_sem=recv, device_id=to, device_id_type=MESH
    )
    copy.start()
    return copy


def landed(ref, send, recv, to):
    pltpu.make_async_remote_copy(
        src_ref=ref, dst_ref=ref, send_sem=send, recv_sem=recv, device_id=to, device_id_type=MESH
    ).wait_recv()


def greet(peers):
    barrier = pltpu.get_barrier_semaphore()
    for peer in peers:
        pl.semaphore_signal(barrier, inc=1, device_id=peer, device_id_type=MESH)
    pl.semaphore_wait(barrier, len(peers))


def plane_peers(a, z, c, p, naux):
    return [
        device((a + da) % naux, z, c, (p + dp) % 2)
        for da in range(naux)
        for dp in range(2)
        if (da, dp) != (0, 0)
    ]


class Ring:
    def __init__(self, block, half, z, nz, c, me, sems):
        self.block, self.half, self.z, self.nz, self.c = block, half, z, nz, c
        self.me = me
        self.up_send, self.up_recv, self.dn_send, self.dn_recv, self.co_send, self.co_recv = sems
        self.up, self.dn, self.co = me(1, 0), me(-1, 0), me(0, 1)
        self.far = nz // 2
        self.sent = []

    def piece(self, way, step, core):
        origin = (self.z - way * (step + 1) + self.nz) % self.nz
        if step + 1 == self.far:
            return self.half(origin, core, 0 if way > 0 else 1)
        return self.block(origin, core)

    def start(self, source, source_halves):
        mine = self.block(self.z, self.c)
        if self.far == 1:
            raise ValueError("short ring")
        self.sent.append(push(source, mine, self.up_send.at[0], self.up_recv.at[0], self.up))
        self.sent.append(push(source, mine, self.dn_send.at[0], self.dn_recv.at[0], self.dn))
        self.sent.append(push(source, mine, self.co_send.at[0], self.co_recv.at[0], self.co))

    def step(self, step):
        for way, send, recv, to in (
            (1, self.up_send, self.up_recv, self.up),
            (-1, self.dn_send, self.dn_recv, self.dn),
        ):
            got = self.piece(way, step, self.c)
            landed(got, send.at[step], recv.at[step], to)
            if step + 1 < self.far:
                onward = got
                if step + 2 == self.far:
                    origin = (self.z - way * (step + 1) + self.nz) % self.nz
                    onward = self.half(origin, self.c, 0 if way > 0 else 1)
                self.sent.append(push(onward, onward, send.at[step + 1], recv.at[step + 1], to))
            k = 1 + 2 * step + (0 if way > 0 else 1)
            self.sent.append(push(got, got, self.co_send.at[k], self.co_recv.at[k], self.co))

    def finish(self):
        other = 1 - self.c
        landed(self.block(self.z, other), self.co_send.at[0], self.co_recv.at[0], self.co)
        for step in range(self.far):
            for way in (1, -1):
                k = 1 + 2 * step + (0 if way > 0 else 1)
                landed(self.piece(way, step, other), self.co_send.at[k], self.co_recv.at[k], self.co)
        for copy in self.sent:
            copy.wait_send()


def ring_sems(nz):
    far = nz // 2
    return [pltpu.SemaphoreType.DMA((far,))] * 4 + [pltpu.SemaphoreType.DMA((1 + 2 * far,))] * 2


def spread_kernel(
    naux, nz, second, first, sec, firstz, firsta, a_send, a_recv, b_send, b_recv, loc, *sems
):
    a, z, c, p = place()
    x, yh = a // 2, a % 2

    def me(dz, dc):
        return device(a, (z + dz + nz) % nz, (c + dc) % 2, p)

    in_plane = plane_peers(a, z, c, p, naux)
    greet(in_plane + [me(1, 0), me(-1, 0), me(0, 1)])

    locals_ = [
        pltpu.make_async_copy(first, firstz.at[:, a], loc.at[0]),
        pltpu.make_async_copy(first, firsta.at[:, z * 2 + c], loc.at[1]),
        pltpu.make_async_copy(second.at[a, :, p], sec.at[:, a * 2 + p], loc.at[2]),
    ]
    sent = []
    right = device((x + 1) % NX * 2 + yh, z, c, p)
    left = device((x + NX - 1) % NX * 2 + yh, z, c, p)
    across = device(x * 2 + (1 - yh), z, c, 1 - p)
    beside = device(a, z, c, 1 - p)
    al = (x + NX - 1) % NX * 2 + yh
    ar = (x + 1) % NX * 2 + yh
    af = (x + 2) % NX * 2 + yh
    sent.append(push(first, firstz.at[:, a], b_send.at[0], b_recv.at[0], right))
    sent.append(push(first, firstz.at[:, a], b_send.at[1], b_recv.at[1], left))
    sent.append(push(first.at[p], firstz.at[p, a], b_send.at[4], b_recv.at[4], across))
    ring = Ring(
        lambda zz, cc: firsta.at[:, zz * 2 + cc],
        lambda zz, cc, h: firsta.at[h, zz * 2 + cc],
        z, nz, c, me, sems,
    )
    ring.start(first, None)
    n = 0
    for da in range(naux):
        for dp in range(2):
            if (da, dp) != (0, 0):
                ta, tp = (a + da) % naux, (p + dp) % 2
                sent.append(
                    push(second.at[ta, :, tp], sec.at[:, a * 2 + p], a_send.at[n], a_recv.at[n],
                         device(ta, z, c, tp))
                )
                n += 1
    for copy in locals_:
        copy.start()

    landed(firstz.at[:, al], b_send.at[0], b_recv.at[0], left)
    sent.append(push(firstz.at[0, al], firstz.at[0, al], b_send.at[2], b_recv.at[2], right))
    sent.append(push(firstz.at[p, al], firstz.at[p, al], b_send.at[5], b_recv.at[5], across))
    landed(firstz.at[:, ar], b_send.at[1], b_recv.at[1], right)
    sent.append(push(firstz.at[1, ar], firstz.at[1, ar], b_send.at[3], b_recv.at[3], left))
    sent.append(push(firstz.at[p, ar], firstz.at[p, ar], b_send.at[6], b_recv.at[6], across))
    ring.step(0)

    def relay(k, slot):
        got = firstz.at[1 - p, slot // 2 * 2 + (1 - yh)]
        landed(got, b_send.at[4 + k], b_recv.at[4 + k], across)
        sent.append(push(got, got, b_send.at[8 + k], b_recv.at[8 + k], beside))

    relay(0, a)
    landed(firstz.at[0, af], b_send.at[2], b_recv.at[2], left)
    landed(firstz.at[1, af], b_send.at[3], b_recv.at[3], right)
    sent.append(push(firstz.at[p, af], firstz.at[p, af], b_send.at[7], b_recv.at[7], across))
    ring.step(1)
    relay(1, al)
    relay(2, ar)
    ring.step(2)
    relay(3, af)
    ring.step(3)
    for k, slot in enumerate((a, al, ar, af)):
        got = firstz.at[p, slot // 2 * 2 + (1 - yh)]
        landed(got, b_send.at[8 + k], b_recv.at[8 + k], beside)
    ring.finish()
    n = 0
    for da in range(naux):
        for dp in range(2):
            if (da, dp) != (0, 0):
                fa, fp = (a - da + naux) % naux, (p + dp) % 2
                landed(sec.at[:, fa * 2 + fp], a_send.at[n], a_recv.at[n], device(fa, z, c, fp))
                n += 1
    for copy in sent:
        copy.wait_send()
    for copy in locals_:
        copy.wait()


def spread(second, first, naux, nz):
    _, _, _, rows, width = second.shape
    ni, frows, _ = first.shape
    return pl.pallas_call(
        functools.partial(spread_kernel, naux, nz),
        out_shape=[
            jax.ShapeDtypeStruct((2, naux * 2, rows, width), BF16),
            jax.ShapeDtypeStruct((ni, naux, frows, width), BF16),
            jax.ShapeDtypeStruct((ni, nz * 2, frows, width), BF16),
        ],
        in_specs=[pl.BlockSpec(memory_space=pl.ANY)] * 2,
        out_specs=[pl.BlockSpec(memory_space=pl.ANY)] * 3,
        scratch_shapes=[
            pltpu.SemaphoreType.DMA((naux * 2 - 1,)),
            pltpu.SemaphoreType.DMA((naux * 2 - 1,)),
            pltpu.SemaphoreType.DMA((12,)),
            pltpu.SemaphoreType.DMA((12,)),
            pltpu.SemaphoreType.DMA((3,)),
            *ring_sems(nz),
        ],
        compiler_params=pltpu.CompilerParams(
            collective_id=1, has_side_effects=True, vmem_limit_bytes=VMEM_LIMIT
        ),
        name="spread",
    )(second, first)


def tile_of(ref, lead, block):
    return ref[(*lead, slice(None), pl.ds(pl.multiple_of(block // 2 * LANES, LANES), LANES))]


def cross_kernel(group, nb, kept, sec, first, own, other):
    i, g = pl.program_id(0), pl.program_id(1)
    lane = lax.broadcasted_iota(jnp.int32, (BLK, LANES), 1)
    for pairs in range(group // 2):
        left = first[0, :, pairs * LANES:(pairs + 1) * LANES].T
        for side, out in ((0, own), (1, other)):
            for e in range(2):
                entry = pairs * 2 + e
                at = ((side * 2 + i) * nb + g * group + entry) * 2
                b0, b1 = kept[at], kept[at + 1]
                which = kept[4 * nb * 2] if side == 0 else 1 - kept[4 * nb * 2]
                right = jnp.concatenate(
                    [tile_of(sec, (which,), b0), tile_of(sec, (which,), b1)], axis=1
                )
                prod = lax.dot_general(
                    left[e * BLK:(e + 1) * BLK], right, (((1,), (0,)), ((), ())),
                    preferred_element_type=F32,
                )
                u0, u1 = prod[:, :LANES], prod[:, LANES:]
                r0 = jnp.where(b0 % 2 == 0, u0, pltpu.roll(u0, BLK, 1))
                r1 = jnp.where(b1 % 2 == 1, u1, pltpu.roll(u1, BLK, 1))
                out[entry] = jnp.where(lane < BLK, r0, r1).astype(out.dtype)


def cross(kept, sec, first, group=8):
    _, rows, width = sec.shape
    ni = first.shape[0]
    nb = width // BLK
    groups = nb // group
    entries = ni * nb
    return pl.pallas_call(
        functools.partial(cross_kernel, group, nb),
        out_shape=[
            jax.ShapeDtypeStruct((entries, BLK, LANES), F32),
            jax.ShapeDtypeStruct((entries, BLK, LANES), BF16),
        ],
        grid_spec=pltpu.PrefetchScalarGridSpec(
            num_scalar_prefetch=1,
            grid=(ni, groups),
            in_specs=[
                pl.BlockSpec((2, rows, width), lambda i, g, kept: (0, 0, 0)),
                pl.BlockSpec((1, rows, group * BLK), lambda i, g, kept: (i, 0, g)),
            ],
            out_specs=[
                pl.BlockSpec((group, BLK, LANES), lambda i, g, kept: (i * groups + g, 0, 0)),
                pl.BlockSpec((group, BLK, LANES), lambda i, g, kept: (i * groups + g, 0, 0)),
            ],
        ),
        compiler_params=pltpu.CompilerParams(vmem_limit_bytes=VMEM_LIMIT),
        name="cross",
    )(kept, sec, first)


def amplitude_kernel(
    naux, nz, own, other, divisor, amp1, amp2,
    twin, pairsum, got, shard, d_send, d_recv, r_send, r_recv, t_send, t_recv, x_send, x_recv,
    loc, *sems
):
    a, z, c, p = place()
    size = divisor.shape[0]

    def me(dz, dc):
        return device(a, (z + dz) % nz, (c + dc) % 2, p)

    sibling = me(0, 1)
    mirror = device(z, a, c, p)
    line = [device((a + da) % naux, z, c, p) for da in range(1, naux)]
    barrier = pltpu.get_barrier_semaphore()
    peers = [sibling] + [me(dz, 0) for dz in range(1, nz)] + line
    for peer in peers:
        pl.semaphore_signal(barrier, inc=1, device_id=peer, device_id_type=MESH)

    @pl.when(a != z)
    def _():
        pl.semaphore_signal(barrier, inc=1, device_id=mirror, device_id_type=MESH)
        pl.semaphore_wait(barrier, len(peers) + 1)

    @pl.when(a == z)
    def _():
        pl.semaphore_wait(barrier, len(peers))

    def rows(t):
        return pl.ds(t * size, size)

    order = sorted(range(nz), key=lambda d: (-min(d, nz - d), d))
    sent = []
    for dz in order:
        part = rows((z + dz) % nz)
        sent.append(push(other.at[part], twin.at[part], d_send.at[dz], d_recv.at[dz], sibling))
    for dz in order:
        t = (z + dz) % nz
        landed(twin.at[rows(t)], d_send.at[dz], d_recv.at[dz], sibling)
        if dz == 0:
            continue

        def add(k, _):
            n = t * size + k
            pairsum[n] = (own[n] + twin[n].astype(F32)).astype(BF16)
            return 0

        lax.fori_loop(0, size, add, 0)
        sent.append(push(pairsum.at[rows(t)], got.at[dz], r_send.at[dz], r_recv.at[dz], me(dz, 0)))
    for dz in range(1, nz):
        landed(got.at[dz], r_send.at[dz], r_recv.at[dz], me(nz - dz, 0))

    def reduce(k, _):
        n = z * size + k
        total = own[n] + twin[n].astype(F32)
        for dz in range(1, nz):
            total = total + got[dz, k].astype(F32)
        shard[k] = (total / divisor[k]).astype(BF16)
        return 0

    lax.fori_loop(0, size, reduce, 0)

    half = size // 2
    ring = Ring(
        lambda zz, cc: amp1.at[cc, pl.ds(zz * size, size)],
        lambda zz, cc, h: amp1.at[cc, pl.ds(zz * size + h * half, half)],
        z, nz, c, lambda dz, dc: me((dz + nz) % nz, dc), sems,
    )

    @pl.when(a != z)
    def _():
        push(shard, amp2.at[rows(z)], t_send.at[0], t_recv.at[0], mirror)

    @pl.when(a == z)
    def _():
        pltpu.make_async_copy(shard, amp2.at[rows(z)], loc.at[0]).start()

    ring.start(shard, None)
    here = pltpu.make_async_copy(shard, amp1.at[c, rows(z)], loc.at[1])
    here.start()

    @pl.when(a != z)
    def _():
        landed(amp2.at[rows(a)], t_send.at[0], t_recv.at[0], mirror)

    @pl.when(a == z)
    def _():
        pltpu.make_async_copy(shard, amp2.at[rows(z)], loc.at[0]).wait()

    for k, peer in enumerate(line):
        sent.append(push(amp2.at[rows(a)], amp2.at[rows(a)], x_send.at[k], x_recv.at[k], peer))
    for step in range(nz // 2):
        ring.step(step)
    for k in range(naux - 1):
        fa = (a - (k + 1) + naux) % naux
        landed(amp2.at[rows(fa)], x_send.at[k], x_recv.at[k], device(fa, z, c, p))
    ring.finish()
    here.wait()
    for copy in sent:
        copy.wait_send()

    @pl.when(a != z)
    def _():
        pltpu.make_async_remote_copy(
            src_ref=shard, dst_ref=amp2.at[rows(z)], send_sem=t_send.at[0], recv_sem=t_recv.at[0],
            device_id=mirror, device_id_type=MESH,
        ).wait_send()


def amplitudes(own, other, divisor, naux, nz):
    entries, rows, lanes = own.shape
    size = divisor.shape[0]
    dma = pltpu.SemaphoreType.DMA
    return pl.pallas_call(
        functools.partial(amplitude_kernel, naux, nz),
        out_shape=[
            jax.ShapeDtypeStruct((2, entries, rows, lanes), BF16),
            jax.ShapeDtypeStruct((entries, rows, lanes), BF16),
        ],
        in_specs=[
            pl.BlockSpec(memory_space=pltpu.VMEM),
            pl.BlockSpec(memory_space=pl.ANY),
            pl.BlockSpec(memory_space=pltpu.VMEM),
        ],
        out_specs=[pl.BlockSpec(memory_space=pl.ANY)] * 2,
        scratch_shapes=[
            pltpu.VMEM((entries, rows, lanes), BF16),
            pltpu.VMEM((entries, rows, lanes), BF16),
            pltpu.VMEM((nz, size, rows, lanes), BF16),
            pltpu.VMEM((size, rows, lanes), BF16),
            dma((nz,)), dma((nz,)), dma((nz,)), dma((nz,)), dma((1,)), dma((1,)),
            dma((naux - 1,)), dma((naux - 1,)), dma((2,)),
            *ring_sems(nz),
        ],
        compiler_params=pltpu.CompilerParams(
            collective_id=2, has_side_effects=True, vmem_limit_bytes=VMEM_LIMIT
        ),
        name="amplitudes",
    )(own, other, divisor)


def spread_halves(amp, b0, b1):
    lane = lax.broadcasted_iota(jnp.int32, (BLK, LANES), 1) // BLK
    turned = pltpu.roll(amp, BLK, 1)
    zero = jnp.zeros_like(amp)
    t0 = jnp.where(lane == b0 % 2, jnp.where(b0 % 2 == 0, amp, turned), zero)
    t1 = jnp.where(lane == b1 % 2, jnp.where(b1 % 2 == 1, amp, turned), zero)
    return t0, t1


def toward_first_kernel(group, nb, kept, sec, amp, out):
    i, g = pl.program_id(0), pl.program_id(1)
    for pairs in range(group // 2):
        halves = []
        for e in range(2):
            entry = pairs * 2 + e
            tiles, weights = [], []
            for core in range(2):
                side = jnp.where(kept[4 * nb * 2] == core, 0, 1)
                at = ((side * 2 + i) * nb + g * group + entry) * 2
                b0, b1 = kept[at], kept[at + 1]
                tiles += [tile_of(sec, (core,), b0), tile_of(sec, (core,), b1)]
                weights += spread_halves(amp[core, entry].astype(F32), b0, b1)
            halves.append(
                lax.dot_general(
                    jnp.concatenate(tiles, axis=1),
                    jnp.concatenate(weights, axis=1).astype(BF16),
                    (((1,), (1,)), ((), ())),
                    preferred_element_type=F32,
                )
            )
        out[0, :, pairs * LANES:(pairs + 1) * LANES] = jnp.concatenate(halves, axis=1).astype(BF16)


def toward_first(kept, sec, amp, ni, group=8):
    _, rows, width = sec.shape
    nb = width // BLK
    groups = nb // group
    return pl.pallas_call(
        functools.partial(toward_first_kernel, group, nb),
        out_shape=jax.ShapeDtypeStruct((ni, rows, width), BF16),
        grid_spec=pltpu.PrefetchScalarGridSpec(
            num_scalar_prefetch=1,
            grid=(ni, groups),
            in_specs=[
                pl.BlockSpec((2, rows, width), lambda i, g, kept: (0, 0, 0)),
                pl.BlockSpec((2, group, BLK, LANES), lambda i, g, kept: (0, i * groups + g, 0, 0)),
            ],
            out_specs=pl.BlockSpec((1, rows, group * BLK), lambda i, g, kept: (i, 0, g)),
        ),
        compiler_params=pltpu.CompilerParams(vmem_limit_bytes=VMEM_LIMIT),
        name="toward_first",
    )(kept, sec, amp)


def toward_second_kernel(group, nb, kept, first, amp, out, total):
    i, g = pl.program_id(0), pl.program_id(1)

    @pl.when((i == 0) & (g == 0))
    def _():
        total[...] = jnp.zeros_like(total)

    nothing = jnp.zeros((BLK, 2 * LANES), BF16)
    for pairs in range(group // 2):
        left = first[0, :, pairs * LANES:(pairs + 1) * LANES]
        for e in range(2):
            entry = pairs * 2 + e
            at = (i * nb + g * group + entry) * 2
            b0, b1 = kept[at], kept[at + 1]
            t0, t1 = spread_halves(amp[entry].astype(F32), b0, b1)
            weights = jnp.concatenate([t0, t1], axis=1).astype(BF16)
            stack = [weights, nothing] if e == 0 else [nothing, weights]
            term = jnp.dot(left, jnp.concatenate(stack, axis=0), preferred_element_type=F32)
            for b, part in ((b0, term[:, :LANES]), (b1, term[:, LANES:])):
                at_lanes = pl.ds(pl.multiple_of(b // 2 * LANES, LANES), LANES)
                total[:, at_lanes] += part

    @pl.when((i == pl.num_programs(0) - 1) & (g == pl.num_programs(1) - 1))
    def _():
        out[...] = total[...].astype(BF16)


def toward_second(kept, first, amp, group=8):
    ni, rows, width = first.shape
    nb = width // BLK
    groups = nb // group
    return pl.pallas_call(
        functools.partial(toward_second_kernel, group, nb),
        out_shape=jax.ShapeDtypeStruct((rows, width), BF16),
        grid_spec=pltpu.PrefetchScalarGridSpec(
            num_scalar_prefetch=1,
            grid=(ni, groups),
            in_specs=[
                pl.BlockSpec((1, rows, group * BLK), lambda i, g, kept: (i, 0, g)),
                pl.BlockSpec((group, BLK, LANES), lambda i, g, kept: (i * groups + g, 0, 0)),
            ],
            out_specs=pl.BlockSpec((rows, width), lambda i, g, kept: (0, 0)),
            scratch_shapes=[pltpu.VMEM((rows, width), F32)],
        ),
        compiler_params=pltpu.CompilerParams(vmem_limit_bytes=VMEM_LIMIT),
        name="toward_second",
    )(kept, first, amp)


def gather_first_kernel(naux, nz, part, out, got, done, a_send, a_recv, z_send, z_recv, loc):
    a, z, c, p = place()
    width = out.shape[2]
    in_plane = plane_peers(a, z, c, p, naux)
    column = [(dz, dc) for dz in range(nz) for dc in range(2) if (dz, dc) != (0, 0)]

    def me(dz, dc):
        return device(a, (z + dz) % nz, (c + dc) % 2, p)

    greet(in_plane + [me(dz, dc) for dz, dc in column])
    here = pltpu.make_async_copy(part.at[p, a], got.at[0], loc.at[0])
    here.start()
    sent = []
    n = 0
    for da in range(naux):
        for dp in range(2):
            if (da, dp) != (0, 0):
                ta, tp = (a + da) % naux, (p + dp) % 2
                n += 1
                sent.append(
                    push(part.at[tp, ta], got.at[n], a_send.at[n], a_recv.at[n], device(ta, z, c, tp))
                )
    n = 0
    for da in range(naux):
        for dp in range(2):
            if (da, dp) != (0, 0):
                n += 1
                fa, fp = (a - da + naux) % naux, (p + dp) % 2
                landed(got.at[n], a_send.at[n], a_recv.at[n], device(fa, z, c, fp))
    here.wait()
    step = 2 * width

    def add(k, _):
        cols = pl.ds(pl.multiple_of(k * step, step), step)
        total = got[0, :, cols].astype(F32)
        for n in range(1, 2 * naux):
            total = total + got[n, :, cols].astype(F32)
        done[:, cols] = total.astype(BF16)
        return 0

    lax.fori_loop(0, nz, add, 0)

    def columns(to_z, to_c):
        return pl.ds(pl.multiple_of((to_z * 2 + to_c) * width, width), width)

    mine = pltpu.make_async_copy(done.at[:, columns(z, c)], out.at[z * 2 + c], loc.at[1])
    mine.start()
    for n, (dz, dc) in enumerate(column):
        tz, tc = (z + dz) % nz, (c + dc) % 2
        sent.append(
            push(done.at[:, columns(tz, tc)], out.at[z * 2 + c], z_send.at[n], z_recv.at[n],
                 device(a, tz, tc, p))
        )
    for n, (dz, dc) in enumerate(column):
        fz, fc = (z - dz + nz) % nz, (c + dc) % 2
        landed(out.at[fz * 2 + fc], z_send.at[n], z_recv.at[n], device(a, fz, fc, p))
    mine.wait()
    for copy in sent:
        copy.wait_send()


def gather_first(part, naux, nz):
    _, _, rows, width = part.shape
    dma = pltpu.SemaphoreType.DMA
    return pl.pallas_call(
        functools.partial(gather_first_kernel, naux, nz),
        out_shape=jax.ShapeDtypeStruct((nz * 2, rows, width // (nz * 2)), BF16),
        in_specs=[pl.BlockSpec(memory_space=pl.ANY)],
        out_specs=pl.BlockSpec(memory_space=pl.ANY),
        scratch_shapes=[
            pltpu.VMEM((naux * 2, rows, width), BF16),
            pltpu.VMEM((rows, width), BF16),
            dma((naux * 2,)), dma((naux * 2,)), dma((nz * 2,)), dma((nz * 2,)), dma((2,)),
        ],
        compiler_params=pltpu.CompilerParams(
            collective_id=3, has_side_effects=True, vmem_limit_bytes=VMEM_LIMIT
        ),
        name="gather_first",
    )(part)


def shards(first_factors, second_factors, first_energy, second_energy, virtual_energy, kept_blocks):
    naux, nz = lax.axis_size("aux"), lax.axis_size("occ") // 2
    a, z, c, p = place()
    rows, nj, width = second_factors.shape
    frows, ni, _ = first_factors.shape
    nb = width // BLK
    entries = ni * nb

    order = [
        (aa * 2 * nz + zz * 2 + cc, zz * 2 * nz + aa * 2 + cc)
        for aa in range(naux) for zz in range(nz) for cc in range(2)
    ]
    kept_here = kept_blocks[:, 0].reshape(entries * 2)
    kept_mine = lax.ppermute(kept_here, ("aux", "occ"), order)
    energy_mine = lax.ppermute(second_energy, ("aux", "occ"), order)
    swap = [(o, o // 2 * 2 + 1 - o % 2) for o in range(2 * nz)]
    kept_twin = lax.ppermute(kept_mine, "occ", swap)
    kept = jnp.concatenate([kept_mine, kept_twin, jnp.full((8,), c, jnp.int32)])

    size = entries // nz
    energy_blocks = virtual_energy.reshape(nb, BLK)
    picked = lax.dynamic_slice_in_dim(kept_mine, z * size * 2, size * 2, 0)
    entry = z * size + jnp.arange(size)
    left = jnp.take(energy_blocks, entry % nb, axis=0)
    right = jnp.take(energy_blocks, picked, axis=0).reshape(size, 2 * BLK)
    low = jnp.take(first_energy, entry // nb)
    divisor = left[:, :, None] + right[:, None, :] - low[:, None, None] - energy_mine[0]

    second = jnp.transpose(second_factors, (1, 0, 2)).reshape(naux, 2, 2, rows, width)
    first = jnp.transpose(first_factors, (1, 0, 2))
    sec, firstz, firsta = spread(second, first, naux, nz)
    sec = sec.reshape(2, naux * 2 * rows, width)
    firstz = firstz.reshape(ni, naux * frows, width)
    firsta = firsta.reshape(ni, nz * 2 * frows, width)

    own, other = cross(kept, sec, firstz)
    amp1, amp2 = amplitudes(own, other, divisor, naux, nz)
    part = toward_first(kept, sec, amp1, ni)
    first_density = gather_first(part.reshape(ni, naux, frows, width), naux, nz)
    second_density = toward_second(kept_here, firsta, amp2)
    return (
        first_density.reshape(nz * 2 * frows, 1, width // (nz * 2)),
        second_density.reshape(nz * 2 * frows, 1, width),
    )


def solution(mesh):
    placed = (
        P(("aux", "occ"), None, None),
        P(("aux", "occ", "pair"), None, None),
        P(),
        P(("occ", "pair")),
        P(),
        P(None, ("occ", "pair"), None, None),
    )
    return jax.shard_map(
        shards,
        mesh=mesh,
        in_specs=placed,
        out_specs=(P("aux", "pair", "occ"), P("aux", ("occ", "pair"), None)),
        check_vma=False,
    )
```

```python
import functools

import jax
import jax.numpy as jnp
from jax import lax
from jax.experimental import pallas as pl
from jax.experimental.pallas import tpu as pltpu
from jax.sharding import PartitionSpec as P

MESH = pl.DeviceIdType.MESH
F32 = jnp.float32
BF16 = jnp.bfloat16
BLK = 64
LANES = 128
NX = 4
ORDER = (
    (1, 0), (0, 1), (3, 0), (0, 3), (1, 1), (3, 3), (1, 3), (3, 1),
    (2, 0), (0, 2), (2, 1), (1, 2), (2, 3), (3, 2), (2, 2),
)
VMEM_LIMIT = 52 * 1024 * 1024


def place():
    aux, occ, pair = lax.axis_index("aux"), lax.axis_index("occ"), lax.axis_index("pair")
    return aux, occ // 2, occ % 2, pair


def device(aux, z, core, pair):
    return {"aux": aux, "occ": z * 2 + core, "pair": pair}


def push(src, dst, send, recv, to):
    copy = pltpu.make_async_remote_copy(
        src_ref=src, dst_ref=dst, send_sem=send, recv_sem=recv, device_id=to, device_id_type=MESH
    )
    copy.start()
    return copy


def landed(ref, send, recv, to):
    pltpu.make_async_remote_copy(
        src_ref=ref, dst_ref=ref, send_sem=send, recv_sem=recv, device_id=to, device_id_type=MESH
    ).wait_recv()


def greet(peers):
    barrier = pltpu.get_barrier_semaphore()
    for peer in peers:
        pl.semaphore_signal(barrier, inc=1, device_id=peer, device_id_type=MESH)
    pl.semaphore_wait(barrier, len(peers))


def plane_peers(a, z, c, p, naux):
    return [
        device((a + da) % naux, z, c, (p + dp) % 2)
        for da in range(naux)
        for dp in range(2)
        if (da, dp) != (0, 0)
    ]


class Ring:
    def __init__(self, block, half, z, nz, c, me, sems):
        self.block, self.half, self.z, self.nz, self.c = block, half, z, nz, c
        self.me = me
        self.up_send, self.up_recv, self.dn_send, self.dn_recv, self.co_send, self.co_recv = sems
        self.up, self.dn, self.co = me(1, 0), me(-1, 0), me(0, 1)
        self.far = nz // 2
        self.sent = []

    def piece(self, way, step, core):
        origin = (self.z - way * (step + 1) + self.nz) % self.nz
        if step + 1 == self.far:
            return self.half(origin, core, 0 if way > 0 else 1)
        return self.block(origin, core)

    def start(self, source, source_halves):
        mine = self.block(self.z, self.c)
        if self.far == 1:
            raise ValueError("short ring")
        self.sent.append(push(source, mine, self.up_send.at[0], self.up_recv.at[0], self.up))
        self.sent.append(push(source, mine, self.dn_send.at[0], self.dn_recv.at[0], self.dn))
        self.sent.append(push(source, mine, self.co_send.at[0], self.co_recv.at[0], self.co))

    def step(self, step):
        for way, send, recv, to in (
            (1, self.up_send, self.up_recv, self.up),
            (-1, self.dn_send, self.dn_recv, self.dn),
        ):
            got = self.piece(way, step, self.c)
            landed(got, send.at[step], recv.at[step], to)
            if step + 1 < self.far:
                onward = got
                if step + 2 == self.far:
                    origin = (self.z - way * (step + 1) + self.nz) % self.nz
                    onward = self.half(origin, self.c, 0 if way > 0 else 1)
                self.sent.append(push(onward, onward, send.at[step + 1], recv.at[step + 1], to))
            k = 1 + 2 * step + (0 if way > 0 else 1)
            self.sent.append(push(got, got, self.co_send.at[k], self.co_recv.at[k], self.co))

    def finish(self):
        other = 1 - self.c
        landed(self.block(self.z, other), self.co_send.at[0], self.co_recv.at[0], self.co)
        for step in range(self.far):
            for way in (1, -1):
                k = 1 + 2 * step + (0 if way > 0 else 1)
                landed(self.piece(way, step, other), self.co_send.at[k], self.co_recv.at[k], self.co)
        for copy in self.sent:
            copy.wait_send()


def ring_sems(nz):
    far = nz // 2
    return [pltpu.SemaphoreType.DMA((far,))] * 4 + [pltpu.SemaphoreType.DMA((1 + 2 * far,))] * 2


def spread_kernel(
    naux, nz, second, first, sec, firstz, firsta, a_send, a_recv, b_send, b_recv, loc, *sems
):
    a, z, c, p = place()
    x, yh = a // 2, a % 2

    def me(dz, dc):
        return device(a, (z + dz + nz) % nz, (c + dc) % 2, p)

    in_plane = plane_peers(a, z, c, p, naux)
    greet(in_plane + [me(1, 0), me(-1, 0), me(0, 1)])

    locals_ = [
        pltpu.make_async_copy(first, firstz.at[:, a], loc.at[0]),
        pltpu.make_async_copy(first, firsta.at[:, z * 2 + c], loc.at[1]),
        pltpu.make_async_copy(second.at[a, :, p], sec.at[:, a * 2 + p], loc.at[2]),
    ]
    sent = []
    right = device((x + 1) % NX * 2 + yh, z, c, p)
    left = device((x + NX - 1) % NX * 2 + yh, z, c, p)
    across = device(x * 2 + (1 - yh), z, c, 1 - p)
    beside = device(a, z, c, 1 - p)
    al = (x + NX - 1) % NX * 2 + yh
    ar = (x + 1) % NX * 2 + yh
    af = (x + 2) % NX * 2 + yh
    sent.append(push(first, firstz.at[:, a], b_send.at[0], b_recv.at[0], right))
    sent.append(push(first, firstz.at[:, a], b_send.at[1], b_recv.at[1], left))
    sent.append(push(first.at[p], firstz.at[p, a], b_send.at[4], b_recv.at[4], across))
    ring = Ring(
        lambda zz, cc: firsta.at[:, zz * 2 + cc],
        lambda zz, cc, h: firsta.at[h, zz * 2 + cc],
        z, nz, c, me, sems,
    )
    ring.start(first, None)
    y = yh * 2 + p
    batches = [4, 2, 3, 2, 2, 2]

    def plane(dx, dy):
        ty = (y + dy) % 4
        return (x + dx) % NX * 2 + ty // 2, ty % 2

    def send_some():
        for _ in range(batches.pop(0) if batches else 0):
            n = len(second_sent)
            ta, tp = plane(*ORDER[n])
            second_sent.append(
                push(second.at[ta, :, tp], sec.at[:, a * 2 + p], a_send.at[n], a_recv.at[n],
                     device(ta, z, c, tp))
            )

    second_sent = []
    send_some()
    for copy in locals_:
        copy.start()

    landed(firstz.at[:, al], b_send.at[0], b_recv.at[0], left)
    sent.append(push(firstz.at[0, al], firstz.at[0, al], b_send.at[2], b_recv.at[2], right))
    sent.append(push(firstz.at[p, al], firstz.at[p, al], b_send.at[5], b_recv.at[5], across))
    send_some()
    landed(firstz.at[:, ar], b_send.at[1], b_recv.at[1], right)
    sent.append(push(firstz.at[1, ar], firstz.at[1, ar], b_send.at[3], b_recv.at[3], left))
    sent.append(push(firstz.at[p, ar], firstz.at[p, ar], b_send.at[6], b_recv.at[6], across))
    send_some()
    ring.step(0)
    send_some()

    def relay(k, slot):
        got = firstz.at[1 - p, slot // 2 * 2 + (1 - yh)]
        landed(got, b_send.at[4 + k], b_recv.at[4 + k], across)
        sent.append(push(got, got, b_send.at[8 + k], b_recv.at[8 + k], beside))

    relay(0, a)
    send_some()
    landed(firstz.at[0, af], b_send.at[2], b_recv.at[2], left)
    landed(firstz.at[1, af], b_send.at[3], b_recv.at[3], right)
    sent.append(push(firstz.at[p, af], firstz.at[p, af], b_send.at[7], b_recv.at[7], across))
    send_some()
    ring.step(1)
    relay(1, al)
    relay(2, ar)
    ring.step(2)
    relay(3, af)
    ring.step(3)
    for k, slot in enumerate((a, al, ar, af)):
        got = firstz.at[p, slot // 2 * 2 + (1 - yh)]
        landed(got, b_send.at[8 + k], b_recv.at[8 + k], beside)
    ring.finish()
    for n, (dx, dy) in enumerate(ORDER):
        fa, fp = plane(NX - dx, 4 - dy)
        landed(sec.at[:, fa * 2 + fp], a_send.at[n], a_recv.at[n], device(fa, z, c, fp))
    for copy in second_sent:
        copy.wait_send()
    for copy in sent:
        copy.wait_send()
    for copy in locals_:
        copy.wait()


def spread(second, first, naux, nz):
    _, _, _, rows, width = second.shape
    ni, frows, _ = first.shape
    return pl.pallas_call(
        functools.partial(spread_kernel, naux, nz),
        out_shape=[
            jax.ShapeDtypeStruct((2, naux * 2, rows, width), BF16),
            jax.ShapeDtypeStruct((ni, naux, frows, width), BF16),
            jax.ShapeDtypeStruct((ni, nz * 2, frows, width), BF16),
        ],
        in_specs=[pl.BlockSpec(memory_space=pl.ANY)] * 2,
        out_specs=[pl.BlockSpec(memory_space=pl.ANY)] * 3,
        scratch_shapes=[
            pltpu.SemaphoreType.DMA((naux * 2 - 1,)),
            pltpu.SemaphoreType.DMA((naux * 2 - 1,)),
            pltpu.SemaphoreType.DMA((12,)),
            pltpu.SemaphoreType.DMA((12,)),
            pltpu.SemaphoreType.DMA((3,)),
            *ring_sems(nz),
        ],
        compiler_params=pltpu.CompilerParams(
            collective_id=1, has_side_effects=True, vmem_limit_bytes=VMEM_LIMIT
        ),
        name="spread",
    )(second, first)


def tile_of(ref, lead, block):
    return ref[(*lead, slice(None), pl.ds(pl.multiple_of(block // 2 * LANES, LANES), LANES))]


def cross_kernel(group, nb, kept, sec, first, own, other):
    i, g = pl.program_id(0), pl.program_id(1)
    lane = lax.broadcasted_iota(jnp.int32, (BLK, LANES), 1)
    for pairs in range(group // 2):
        left = first[0, :, pairs * LANES:(pairs + 1) * LANES].T
        for side, out in ((0, own), (1, other)):
            for e in range(2):
                entry = pairs * 2 + e
                at = ((side * 2 + i) * nb + g * group + entry) * 2
                b0, b1 = kept[at], kept[at + 1]
                which = kept[4 * nb * 2] if side == 0 else 1 - kept[4 * nb * 2]
                right = jnp.concatenate(
                    [tile_of(sec, (which,), b0), tile_of(sec, (which,), b1)], axis=1
                )
                prod = lax.dot_general(
                    left[e * BLK:(e + 1) * BLK], right, (((1,), (0,)), ((), ())),
                    preferred_element_type=F32,
                )
                u0, u1 = prod[:, :LANES], prod[:, LANES:]
                r0 = jnp.where(b0 % 2 == 0, u0, pltpu.roll(u0, BLK, 1))
                r1 = jnp.where(b1 % 2 == 1, u1, pltpu.roll(u1, BLK, 1))
                out[entry] = jnp.where(lane < BLK, r0, r1).astype(out.dtype)


def cross(kept, sec, first, group=8):
    _, rows, width = sec.shape
    ni = first.shape[0]
    nb = width // BLK
    groups = nb // group
    entries = ni * nb
    return pl.pallas_call(
        functools.partial(cross_kernel, group, nb),
        out_shape=[
            jax.ShapeDtypeStruct((entries, BLK, LANES), F32),
            jax.ShapeDtypeStruct((entries, BLK, LANES), BF16),
        ],
        grid_spec=pltpu.PrefetchScalarGridSpec(
            num_scalar_prefetch=1,
            grid=(ni, groups),
            in_specs=[
                pl.BlockSpec((2, rows, width), lambda i, g, kept: (0, 0, 0)),
                pl.BlockSpec((1, rows, group * BLK), lambda i, g, kept: (i, 0, g)),
            ],
            out_specs=[
                pl.BlockSpec((group, BLK, LANES), lambda i, g, kept: (i * groups + g, 0, 0)),
                pl.BlockSpec((group, BLK, LANES), lambda i, g, kept: (i * groups + g, 0, 0)),
            ],
        ),
        compiler_params=pltpu.CompilerParams(vmem_limit_bytes=VMEM_LIMIT),
        name="cross",
    )(kept, sec, first)


def amplitude_kernel(
    naux, nz, own, other, divisor, amp1, amp2,
    twin, outgoing, got, shard, d_send, d_recv, r_send, r_recv, t_send, t_recv, loc, *sems
):
    a, z, c, p = place()
    size = divisor.shape[0]

    def me(dz, dc):
        return device(a, (z + dz) % nz, (c + dc) % 2, p)

    sibling = me(0, 1)
    mirror = device(z, a, c, p)
    barrier = pltpu.get_barrier_semaphore()
    peers = [sibling, me(1, 0), me(nz - 1, 0)]
    for peer in peers:
        pl.semaphore_signal(barrier, inc=1, device_id=peer, device_id_type=MESH)

    @pl.when(a != z)
    def _():
        pl.semaphore_signal(barrier, inc=1, device_id=mirror, device_id_type=MESH)
        pl.semaphore_wait(barrier, len(peers) + 1)

    @pl.when(a == z)
    def _():
        pl.semaphore_wait(barrier, len(peers))

    def rows(t):
        return pl.ds(t * size, size)

    far, half = nz // 2, size // 2
    order = sorted(range(nz), key=lambda d: (-min(d, nz - d), d))
    sent = []
    for dz in order:
        part = rows((z + dz) % nz)
        sent.append(push(other.at[part], twin.at[part], d_send.at[dz], d_recv.at[dz], sibling))
    ways = ((1, 0, me(1, 0)), (-1, 1, me(nz - 1, 0)))
    for step in range(far):
        for way, w, to in ways:
            dz = way * (far - step) % nz
            t = (z + dz) % nz
            if step or w == 0:
                landed(twin.at[rows(t)], d_send.at[dz], d_recv.at[dz], sibling)
            first_row = w * half if step == 0 else 0
            count = half if step == 0 else size
            if step:
                before = pl.ds(w * half, half) if step == 1 else pl.ds(0, size)
                come = got.at[w, step - 1, before]
                landed(come, r_send.at[w, step - 1], r_recv.at[w, step - 1], to)

            def add(k, _):
                n = t * size + k
                total = own[n] + twin[n].astype(F32)
                outgoing[w, step, k] = total.astype(BF16)
                return 0

            def add_got(k, _):
                n = t * size + k
                total = own[n] + twin[n].astype(F32) + got[w, step - 1, k].astype(F32)
                outgoing[w, step, k] = total.astype(BF16)
                return 0

            if step == 0:
                lax.fori_loop(first_row, first_row + count, add, 0)
            elif step == 1:
                lax.fori_loop(w * half, w * half + half, add_got, 0)
                lax.fori_loop((1 - w) * half, (1 - w) * half + half, add, 0)
            else:
                lax.fori_loop(0, size, add_got, 0)
            span = pl.ds(first_row, count)
            sent.append(
                push(outgoing.at[w, step, span], got.at[w, step, span],
                     r_send.at[w, step], r_recv.at[w, step], to)
            )
    landed(twin.at[rows(z)], d_send.at[0], d_recv.at[0], sibling)
    for way, w, to in ways:
        landed(got.at[w, far - 1], r_send.at[w, far - 1], r_recv.at[w, far - 1], to)

    def reduce(k, _):
        n = z * size + k
        total = own[n] + twin[n].astype(F32)
        total = total + got[0, far - 1, k].astype(F32) + got[1, far - 1, k].astype(F32)
        shard[k] = (total / divisor[k]).astype(BF16)
        return 0

    lax.fori_loop(0, size, reduce, 0)

    ring = Ring(
        lambda zz, cc: amp1.at[cc, pl.ds(zz * size, size)],
        lambda zz, cc, h: amp1.at[cc, pl.ds(zz * size + h * half, half)],
        z, nz, c, lambda dz, dc: me((dz + nz) % nz, dc), sems,
    )

    @pl.when(a != z)
    def _():
        push(shard, amp2, t_send.at[0], t_recv.at[0], mirror)

    @pl.when(a == z)
    def _():
        pltpu.make_async_copy(shard, amp2, loc.at[0]).start()

    ring.start(shard, None)
    here = pltpu.make_async_copy(shard, amp1.at[c, rows(z)], loc.at[1])
    here.start()

    for step in range(nz // 2):
        ring.step(step)
    ring.finish()

    @pl.when(a != z)
    def _():
        landed(amp2, t_send.at[0], t_recv.at[0], mirror)

    @pl.when(a == z)
    def _():
        pltpu.make_async_copy(shard, amp2, loc.at[0]).wait()

    here.wait()
    for copy in sent:
        copy.wait_send()

    @pl.when(a != z)
    def _():
        pltpu.make_async_remote_copy(
            src_ref=shard, dst_ref=amp2, send_sem=t_send.at[0], recv_sem=t_recv.at[0],
            device_id=mirror, device_id_type=MESH,
        ).wait_send()


def amplitudes(own, other, divisor, naux, nz):
    entries, rows, lanes = own.shape
    size = divisor.shape[0]
    dma = pltpu.SemaphoreType.DMA
    return pl.pallas_call(
        functools.partial(amplitude_kernel, naux, nz),
        out_shape=[
            jax.ShapeDtypeStruct((2, entries, rows, lanes), BF16),
            jax.ShapeDtypeStruct((size, rows, lanes), BF16),
        ],
        in_specs=[
            pl.BlockSpec(memory_space=pltpu.VMEM),
            pl.BlockSpec(memory_space=pl.ANY),
            pl.BlockSpec(memory_space=pltpu.VMEM),
        ],
        out_specs=[pl.BlockSpec(memory_space=pl.ANY)] * 2,
        scratch_shapes=[
            pltpu.VMEM((entries, rows, lanes), BF16),
            pltpu.VMEM((2, nz // 2, size, rows, lanes), BF16),
            pltpu.VMEM((2, nz // 2, size, rows, lanes), BF16),
            pltpu.VMEM((size, rows, lanes), BF16),
            dma((nz,)), dma((nz,)), dma((2, nz // 2)), dma((2, nz // 2)), dma((1,)), dma((1,)),
            dma((2,)),
            *ring_sems(nz),
        ],
        compiler_params=pltpu.CompilerParams(
            collective_id=2, has_side_effects=True, vmem_limit_bytes=VMEM_LIMIT
        ),
        name="amplitudes",
    )(own, other, divisor)


def spread_halves(amp, b0, b1):
    lane = lax.broadcasted_iota(jnp.int32, (BLK, LANES), 1) // BLK
    turned = pltpu.roll(amp, BLK, 1)
    zero = jnp.zeros_like(amp)
    t0 = jnp.where(lane == b0 % 2, jnp.where(b0 % 2 == 0, amp, turned), zero)
    t1 = jnp.where(lane == b1 % 2, jnp.where(b1 % 2 == 1, amp, turned), zero)
    return t0, t1


def toward_first_kernel(group, nb, kept, sec, amp, out):
    i, g = pl.program_id(0), pl.program_id(1)
    naux, _, frows, _ = out.shape
    for pairs in range(group // 2):
        halves = []
        for e in range(2):
            entry = pairs * 2 + e
            tiles, weights = [], []
            for core in range(2):
                side = jnp.where(kept[4 * nb * 2] == core, 0, 1)
                at = ((side * 2 + i) * nb + g * group + entry) * 2
                b0, b1 = kept[at], kept[at + 1]
                tiles += [tile_of(sec, (core,), b0), tile_of(sec, (core,), b1)]
                weights += spread_halves(amp[core, entry].astype(F32), b0, b1)
            halves.append(
                lax.dot_general(
                    jnp.concatenate(tiles, axis=1),
                    jnp.concatenate(weights, axis=1).astype(BF16),
                    (((1,), (1,)), ((), ())),
                    preferred_element_type=F32,
                )
            )
        both = jnp.concatenate(halves, axis=1).astype(BF16)
        out[:, 0, :, pairs * LANES:(pairs + 1) * LANES] = both.reshape(naux, frows, LANES)


def toward_first(kept, sec, amp, ni, naux, group=8):
    _, rows, width = sec.shape
    nb = width // BLK
    groups = nb // group
    return pl.pallas_call(
        functools.partial(toward_first_kernel, group, nb),
        out_shape=jax.ShapeDtypeStruct((naux, ni, rows // naux, width), BF16),
        grid_spec=pltpu.PrefetchScalarGridSpec(
            num_scalar_prefetch=1,
            grid=(ni, groups),
            in_specs=[
                pl.BlockSpec((2, rows, width), lambda i, g, kept: (0, 0, 0)),
                pl.BlockSpec((2, group, BLK, LANES), lambda i, g, kept: (0, i * groups + g, 0, 0)),
            ],
            out_specs=pl.BlockSpec(
                (naux, 1, rows // naux, group * BLK), lambda i, g, kept: (0, i, 0, g)
            ),
        ),
        compiler_params=pltpu.CompilerParams(vmem_limit_bytes=VMEM_LIMIT),
        cost_estimate=pl.CostEstimate(
            flops=ni * nb * BLK * rows * 4 * LANES * 4, bytes_accessed=24 << 20, transcendentals=0
        ),
        name="toward_first",
    )(kept, sec, amp)


def toward_second_kernel(group, nb, kept, first, amp, *rest):
    out, total = rest[-2:]
    i, g = pl.program_id(0), pl.program_id(1)

    @pl.when((i == 0) & (g == 0))
    def _():
        total[...] = jnp.zeros_like(total)

    nothing = jnp.zeros((BLK, 2 * LANES), BF16)
    for pairs in range(group // 2):
        left = first[0, :, pairs * LANES:(pairs + 1) * LANES]
        for e in range(2):
            entry = pairs * 2 + e
            at = (i * nb + g * group + entry) * 2
            b0, b1 = kept[at], kept[at + 1]
            t0, t1 = spread_halves(amp[entry].astype(F32), b0, b1)
            weights = jnp.concatenate([t0, t1], axis=1).astype(BF16)
            stack = [weights, nothing] if e == 0 else [nothing, weights]
            term = jnp.dot(left, jnp.concatenate(stack, axis=0), preferred_element_type=F32)
            for b, part in ((b0, term[:, :LANES]), (b1, term[:, LANES:])):
                at_lanes = pl.ds(pl.multiple_of(b // 2 * LANES, LANES), LANES)
                total[:, at_lanes] += part

    @pl.when((i == pl.num_programs(0) - 1) & (g == pl.num_programs(1) - 1))
    def _():
        out[...] = total[...].astype(BF16)


def toward_second(kept, first, amp, height, place_of, before, group=8):
    ni, rows, width = first.shape
    nb = width // BLK
    groups = nb // group
    in_specs = [
        pl.BlockSpec((1, height, group * BLK), lambda i, g, kept: (i, place_of, g)),
        pl.BlockSpec((group, BLK, LANES), lambda i, g, kept: (i * groups + g, 0, 0)),
    ]
    operands = [kept, first, amp]
    if before is not None:
        in_specs.append(pl.BlockSpec(memory_space=pl.ANY))
        operands.append(before)
    return pl.pallas_call(
        functools.partial(toward_second_kernel, group, nb),
        out_shape=jax.ShapeDtypeStruct((rows, width), BF16),
        grid_spec=pltpu.PrefetchScalarGridSpec(
            num_scalar_prefetch=1,
            grid=(ni, groups),
            in_specs=in_specs,
            out_specs=pl.BlockSpec((height, width), lambda i, g, kept: (place_of, 0)),
            scratch_shapes=[pltpu.VMEM((height, width), F32)],
        ),
        input_output_aliases={} if before is None else {3: 0},
        compiler_params=pltpu.CompilerParams(vmem_limit_bytes=VMEM_LIMIT),
        cost_estimate=pl.CostEstimate(
            flops=ni * nb * BLK * height * 4 * LANES * 4,
            bytes_accessed=height << 18, transcendentals=0
        ),
        name="toward_second",
    )(*operands)


def shards(first_factors, second_factors, first_energy, second_energy, virtual_energy, kept_blocks):
    naux, nz = lax.axis_size("aux"), lax.axis_size("occ") // 2
    a, z, c, p = place()
    rows, nj, width = second_factors.shape
    frows, ni, _ = first_factors.shape
    nb = width // BLK
    entries = ni * nb

    order = [
        (aa * 2 * nz + zz * 2 + cc, zz * 2 * nz + aa * 2 + cc)
        for aa in range(naux) for zz in range(nz) for cc in range(2)
    ]
    kept_here = kept_blocks[:, 0].reshape(entries * 2)
    kept_mine = lax.ppermute(kept_here, ("aux", "occ"), order)
    energy_mine = lax.ppermute(second_energy, ("aux", "occ"), order)
    swap = [(o, o // 2 * 2 + 1 - o % 2) for o in range(2 * nz)]
    kept_twin = lax.ppermute(kept_mine, "occ", swap)
    kept = jnp.concatenate([kept_mine, kept_twin, jnp.full((8,), c, jnp.int32)])

    size = entries // nz
    energy_blocks = virtual_energy.reshape(nb, BLK)
    picked = lax.dynamic_slice_in_dim(kept_mine, z * size * 2, size * 2, 0)
    entry = z * size + jnp.arange(size)
    left = jnp.take(energy_blocks, entry % nb, axis=0)
    right = jnp.take(energy_blocks, picked, axis=0).reshape(size, 2 * BLK)
    low = jnp.take(first_energy, entry // nb)
    divisor = left[:, :, None] + right[:, None, :] - low[:, None, None] - energy_mine[0]

    second = jnp.transpose(second_factors, (1, 0, 2)).reshape(naux, 2, 2, rows, width)
    first = jnp.transpose(first_factors, (1, 0, 2))
    sec, firstz, firsta = spread(second, first, naux, nz)
    sec = sec.reshape(2, naux * 2 * rows, width)
    firstz = firstz.reshape(ni, naux * frows, width)
    firsta = firsta.reshape(ni, nz * 2 * frows, width)

    own, other = cross(kept, sec, firstz)
    amp1, amp2 = amplitudes(own, other, divisor, naux, nz)
    amp2 = jnp.broadcast_to(amp2[None], (naux, *amp2.shape))
    amp2 = lax.all_to_all(amp2, "aux", split_axis=0, concat_axis=0, tiled=True)
    amp2 = amp2.reshape(entries, BLK, LANES)

    part = toward_first(kept, sec, amp1, ni, naux).reshape(naux * ni, frows, width)
    amp2, part = lax.optimization_barrier((amp2, part))
    terms = lax.all_to_all(part, ("aux", "pair"), split_axis=0, concat_axis=0, tiled=True)
    most = nz * frows * 3 // 2
    second_density = toward_second(kept_here, firsta, amp2, most, 0, None)
    terms, second_density = lax.optimization_barrier((terms, second_density))
    done = jnp.sum(terms.astype(F32), axis=0).astype(BF16)
    first_density = lax.all_to_all(done, "occ", split_axis=1, concat_axis=0, tiled=True)
    second_density = toward_second(kept_here, firsta, amp2, most // 3, 3, second_density)
    return (
        first_density.reshape(nz * 2 * frows, 1, width // (nz * 2)),
        second_density.reshape(nz * 2 * frows, 1, width),
    )


def solution(mesh):
    placed = (
        P(("aux", "occ"), None, None),
        P(("aux", "occ", "pair"), None, None),
        P(),
        P(("occ", "pair")),
        P(),
        P(None, ("occ", "pair"), None, None),
    )
    return jax.shard_map(
        shards,
        mesh=mesh,
        in_specs=placed,
        out_specs=(P("aux", "pair", "occ"), P("aux", ("occ", "pair"), None)),
        check_vma=False,
    )
```

```python
import functools

import jax
import jax.numpy as jnp
from jax import lax
from jax.experimental import pallas as pl
from jax.experimental.pallas import tpu as pltpu
from jax.sharding import PartitionSpec as P

MESH = pl.DeviceIdType.MESH
F32 = jnp.float32
BF16 = jnp.bfloat16
BLK = 64
LANES = 128
NX = 4
ORDER = (
    (1, 0), (0, 1), (3, 0), (0, 3), (1, 1), (3, 3), (1, 3), (3, 1),
    (2, 0), (0, 2), (2, 1), (1, 2), (2, 3), (3, 2), (2, 2),
)
LINE = ((1, 0), (3, 0), (0, 1), (2, 0), (1, 1), (3, 1), (2, 1))
VMEM_LIMIT = 52 * 1024 * 1024


def place():
    aux, occ, pair = lax.axis_index("aux"), lax.axis_index("occ"), lax.axis_index("pair")
    return aux, occ // 2, occ % 2, pair


def device(aux, z, core, pair):
    return {"aux": aux, "occ": z * 2 + core, "pair": pair}


def push(src, dst, send, recv, to):
    copy = pltpu.make_async_remote_copy(
        src_ref=src, dst_ref=dst, send_sem=send, recv_sem=recv, device_id=to, device_id_type=MESH
    )
    copy.start()
    return copy


def landed(ref, send, recv, to):
    pltpu.make_async_remote_copy(
        src_ref=ref, dst_ref=ref, send_sem=send, recv_sem=recv, device_id=to, device_id_type=MESH
    ).wait_recv()


def greet(peers):
    barrier = pltpu.get_barrier_semaphore()
    for peer in peers:
        pl.semaphore_signal(barrier, inc=1, device_id=peer, device_id_type=MESH)
    pl.semaphore_wait(barrier, len(peers))


def plane_peers(a, z, c, p, naux):
    return [
        device((a + da) % naux, z, c, (p + dp) % 2)
        for da in range(naux)
        for dp in range(2)
        if (da, dp) != (0, 0)
    ]


class Ring:
    def __init__(self, block, half, z, nz, c, me, sems):
        self.block, self.half, self.z, self.nz, self.c = block, half, z, nz, c
        self.me = me
        self.up_send, self.up_recv, self.dn_send, self.dn_recv, self.co_send, self.co_recv = sems
        self.up, self.dn, self.co = me(1, 0), me(-1, 0), me(0, 1)
        self.far = nz // 2
        self.sent = []

    def piece(self, way, step, core):
        origin = (self.z - way * (step + 1) + self.nz) % self.nz
        if step + 1 == self.far:
            return self.half(origin, core, 0 if way > 0 else 1)
        return self.block(origin, core)

    def start(self, source, source_halves):
        mine = self.block(self.z, self.c)
        if self.far == 1:
            raise ValueError("short ring")
        self.sent.append(push(source, mine, self.up_send.at[0], self.up_recv.at[0], self.up))
        self.sent.append(push(source, mine, self.dn_send.at[0], self.dn_recv.at[0], self.dn))
        self.sent.append(push(source, mine, self.co_send.at[0], self.co_recv.at[0], self.co))

    def step(self, step):
        for way, send, recv, to in (
            (1, self.up_send, self.up_recv, self.up),
            (-1, self.dn_send, self.dn_recv, self.dn),
        ):
            got = self.piece(way, step, self.c)
            landed(got, send.at[step], recv.at[step], to)
            if step + 1 < self.far:
                onward = got
                if step + 2 == self.far:
                    origin = (self.z - way * (step + 1) + self.nz) % self.nz
                    onward = self.half(origin, self.c, 0 if way > 0 else 1)
                self.sent.append(push(onward, onward, send.at[step + 1], recv.at[step + 1], to))
            k = 1 + 2 * step + (0 if way > 0 else 1)
            self.sent.append(push(got, got, self.co_send.at[k], self.co_recv.at[k], self.co))

    def finish(self):
        other = 1 - self.c
        landed(self.block(self.z, other), self.co_send.at[0], self.co_recv.at[0], self.co)
        for step in range(self.far):
            for way in (1, -1):
                k = 1 + 2 * step + (0 if way > 0 else 1)
                landed(self.piece(way, step, other), self.co_send.at[k], self.co_recv.at[k], self.co)
        for copy in self.sent:
            copy.wait_send()


def ring_sems(nz):
    far = nz // 2
    return [pltpu.SemaphoreType.DMA((far,))] * 4 + [pltpu.SemaphoreType.DMA((1 + 2 * far,))] * 2


def spread_kernel(
    naux, nz, second, first, sec, firstz, firsta, a_send, a_recv, b_send, b_recv, loc, *sems
):
    a, z, c, p = place()
    x, yh = a // 2, a % 2

    def me(dz, dc):
        return device(a, (z + dz + nz) % nz, (c + dc) % 2, p)

    in_plane = plane_peers(a, z, c, p, naux)
    greet(in_plane + [me(1, 0), me(-1, 0), me(0, 1)])

    locals_ = [
        pltpu.make_async_copy(first, firstz.at[:, a], loc.at[0]),
        pltpu.make_async_copy(first, firsta.at[:, z * 2 + c], loc.at[1]),
        pltpu.make_async_copy(second.at[a, :, p], sec.at[:, a * 2 + p], loc.at[2]),
    ]
    sent = []
    right = device((x + 1) % NX * 2 + yh, z, c, p)
    left = device((x + NX - 1) % NX * 2 + yh, z, c, p)
    across = device(x * 2 + (1 - yh), z, c, 1 - p)
    beside = device(a, z, c, 1 - p)
    al = (x + NX - 1) % NX * 2 + yh
    ar = (x + 1) % NX * 2 + yh
    af = (x + 2) % NX * 2 + yh
    sent.append(push(first, firstz.at[:, a], b_send.at[0], b_recv.at[0], right))
    sent.append(push(first, firstz.at[:, a], b_send.at[1], b_recv.at[1], left))
    sent.append(push(first.at[p], firstz.at[p, a], b_send.at[4], b_recv.at[4], across))
    ring = Ring(
        lambda zz, cc: firsta.at[:, zz * 2 + cc],
        lambda zz, cc, h: firsta.at[h, zz * 2 + cc],
        z, nz, c, me, sems,
    )
    ring.start(first, None)
    y = yh * 2 + p
    batches = [4, 2, 3, 2, 2, 2]

    def plane(dx, dy):
        ty = (y + dy) % 4
        return (x + dx) % NX * 2 + ty // 2, ty % 2

    def send_some():
        for _ in range(batches.pop(0) if batches else 0):
            n = len(second_sent)
            ta, tp = plane(*ORDER[n])
            second_sent.append(
                push(second.at[ta, :, tp], sec.at[:, a * 2 + p], a_send.at[n], a_recv.at[n],
                     device(ta, z, c, tp))
            )

    second_sent = []
    send_some()
    for copy in locals_:
        copy.start()

    landed(firstz.at[:, al], b_send.at[0], b_recv.at[0], left)
    sent.append(push(firstz.at[0, al], firstz.at[0, al], b_send.at[2], b_recv.at[2], right))
    sent.append(push(firstz.at[p, al], firstz.at[p, al], b_send.at[5], b_recv.at[5], across))
    send_some()
    landed(firstz.at[:, ar], b_send.at[1], b_recv.at[1], right)
    sent.append(push(firstz.at[1, ar], firstz.at[1, ar], b_send.at[3], b_recv.at[3], left))
    sent.append(push(firstz.at[p, ar], firstz.at[p, ar], b_send.at[6], b_recv.at[6], across))
    send_some()
    ring.step(0)
    send_some()

    def relay(k, slot):
        got = firstz.at[1 - p, slot // 2 * 2 + (1 - yh)]
        landed(got, b_send.at[4 + k], b_recv.at[4 + k], across)
        sent.append(push(got, got, b_send.at[8 + k], b_recv.at[8 + k], beside))

    relay(0, a)
    send_some()
    landed(firstz.at[0, af], b_send.at[2], b_recv.at[2], left)
    landed(firstz.at[1, af], b_send.at[3], b_recv.at[3], right)
    sent.append(push(firstz.at[p, af], firstz.at[p, af], b_send.at[7], b_recv.at[7], across))
    send_some()
    ring.step(1)
    relay(1, al)
    relay(2, ar)
    ring.step(2)
    relay(3, af)
    ring.step(3)
    for k, slot in enumerate((a, al, ar, af)):
        got = firstz.at[p, slot // 2 * 2 + (1 - yh)]
        landed(got, b_send.at[8 + k], b_recv.at[8 + k], beside)
    ring.finish()
    for n, (dx, dy) in enumerate(ORDER):
        fa, fp = plane(NX - dx, 4 - dy)
        landed(sec.at[:, fa * 2 + fp], a_send.at[n], a_recv.at[n], device(fa, z, c, fp))
    for copy in second_sent:
        copy.wait_send()
    for copy in sent:
        copy.wait_send()
    for copy in locals_:
        copy.wait()


def spread(second, first, naux, nz):
    _, _, _, rows, width = second.shape
    ni, frows, _ = first.shape
    return pl.pallas_call(
        functools.partial(spread_kernel, naux, nz),
        out_shape=[
            jax.ShapeDtypeStruct((2, naux * 2, rows, width), BF16),
            jax.ShapeDtypeStruct((ni, naux, frows, width), BF16),
            jax.ShapeDtypeStruct((ni, nz * 2, frows, width), BF16),
        ],
        in_specs=[pl.BlockSpec(memory_space=pl.ANY)] * 2,
        out_specs=[pl.BlockSpec(memory_space=pl.ANY)] * 3,
        scratch_shapes=[
            pltpu.SemaphoreType.DMA((naux * 2 - 1,)),
            pltpu.SemaphoreType.DMA((naux * 2 - 1,)),
            pltpu.SemaphoreType.DMA((12,)),
            pltpu.SemaphoreType.DMA((12,)),
            pltpu.SemaphoreType.DMA((3,)),
            *ring_sems(nz),
        ],
        compiler_params=pltpu.CompilerParams(
            collective_id=1, has_side_effects=True, vmem_limit_bytes=VMEM_LIMIT
        ),
        name="spread",
    )(second, first)


def tile_of(ref, lead, block):
    return ref[(*lead, slice(None), pl.ds(pl.multiple_of(block // 2 * LANES, LANES), LANES))]


def load_tiles(sec_hbm, sec, sem):
    return [
        pltpu.make_async_copy(sec_hbm.at[:, :, pl.ds(t * LANES, LANES)], sec.at[:, t], sem.at[t])
        for t in range(sec.shape[1])
    ]


def spread_masked(amp, straight):
    lane = lax.broadcasted_iota(jnp.int32, (BLK, LANES), 1)
    zero = jnp.zeros_like(amp)
    stay = jnp.where(straight, amp, zero)
    move = pltpu.roll(jnp.where(straight, zero, amp), BLK, 1)
    return jnp.where(lane < BLK, stay, move), jnp.where(lane < BLK, move, stay)


def amplitude_kernel(
    naux, nz, nb, tiles, sec_hbm, first_hbm, straight, divisor, amp1, amp2,
    sec, first, own, other, twin, outgoing, got, shard,
    d_send, d_recv, r_send, r_recv, t_send, t_recv, x_send, x_recv, s_load, loc, *sems
):
    a, z, c, p = place()
    x, yh = a // 2, a % 2
    size = divisor.shape[0]
    loads = [pltpu.make_async_copy(first_hbm, first, loc.at[2]), *load_tiles(sec_hbm, sec, s_load)]
    for load in loads:
        load.start()
    far, half = nz // 2, size // 2

    def me(dz, dc):
        return device(a, (z + dz) % nz, (c + dc) % 2, p)

    sibling = me(0, 1)
    mirror = device(z, a, c, p)
    barrier = pltpu.get_barrier_semaphore()
    line = [
        device((x + dx) % NX * 2 + (yh + dy) % 2, z, c, p) for dx, dy in LINE
    ]
    peers = [sibling, me(1, 0), me(nz - 1, 0)] + line
    for peer in peers:
        pl.semaphore_signal(barrier, inc=1, device_id=peer, device_id_type=MESH)

    @pl.when(a != z)
    def _():
        pl.semaphore_signal(barrier, inc=1, device_id=mirror, device_id_type=MESH)
        pl.semaphore_wait(barrier, len(peers) + 1)

    @pl.when(a == z)
    def _():
        pl.semaphore_wait(barrier, len(peers))

    for load in loads:
        load.wait()
    lane = lax.broadcasted_iota(jnp.int32, (BLK, LANES), 1)

    def rows(t):
        return pl.ds(t * size, size)

    sent = []

    def compute(dz):
        t = (z + dz) % nz
        i, start = t * size // nb, t * size % nb

        def two(k, _):
            tile = pl.ds(pl.multiple_of((start // 2 + k) * LANES, LANES), LANES)
            left = first[i, :, tile].T
            for side, out in ((0, own), (1, other)):
                which = c if side == 0 else 1 - c
                for e in range(2):
                    at = (side * 2 + i) * nb + start + k * 2 + e
                    right = jnp.concatenate(
                        [sec[which, tiles[at * 2]], sec[which, tiles[at * 2 + 1]]], axis=1
                    )
                    prod = lax.dot_general(
                        left[e * BLK:(e + 1) * BLK], right, (((1,), (0,)), ((), ())),
                        preferred_element_type=F32,
                    )
                    u0, u1 = prod[:, :LANES], prod[:, LANES:]
                    stay = jnp.where(lane < BLK, u0, u1)
                    move = pltpu.roll(jnp.where(lane < BLK, u1, u0), BLK, 1)
                    chosen = jnp.where(straight[pl.ds(at, 1), :] > 0.5, stay, move)
                    out[t * size + k * 2 + e] = chosen.astype(out.dtype)
            return 0

        lax.fori_loop(0, size // 2, two, 0)
        sent.append(
            push(other.at[rows(t)], twin.at[rows(t)], d_send.at[dz], d_recv.at[dz], sibling)
        )

    ways = ((1, 0, me(1, 0)), (-1, 1, me(nz - 1, 0)))

    def reduce_step(step, way, w, to):
        dz = way * (far - step) % nz
        t = (z + dz) % nz
        if step or w == 0:
            landed(twin.at[rows(t)], d_send.at[dz], d_recv.at[dz], sibling)

        def add(k, _):
            n = t * size + k
            total = own[n] + twin[n].astype(F32)
            outgoing[w, step, k] = total.astype(BF16)
            return 0

        def add_got(k, _):
            n = t * size + k
            total = own[n] + twin[n].astype(F32) + got[w, step - 1, k].astype(F32)
            outgoing[w, step, k] = total.astype(BF16)
            return 0

        for h in (1 - w, w):
            if step == 0 and h != w:
                continue
            span = pl.ds(h * half, half)
            if step > 1 or (step == 1 and h == w):
                landed(got.at[w, step - 1, span], r_send.at[w, step - 1, h],
                       r_recv.at[w, step - 1, h], to)
                lax.fori_loop(h * half, h * half + half, add_got, 0, unroll=4)
            else:
                lax.fori_loop(h * half, h * half + half, add, 0, unroll=4)
            sent.append(
                push(outgoing.at[w, step, span], got.at[w, step, span],
                     r_send.at[w, step, h], r_recv.at[w, step, h], to)
            )

    compute(far)
    compute(far - 1)
    reduce_step(0, *ways[0])
    reduce_step(0, *ways[1])
    for step in range(1, far):
        compute(nz - far + step)
        reduce_step(step, *ways[0])
        compute(far - 1 - step)
        reduce_step(step, *ways[1])

    landed(twin.at[rows(z)], d_send.at[0], d_recv.at[0], sibling)
    for way, w, to in ways:
        for h in range(2):
            landed(got.at[w, far - 1, pl.ds(h * half, half)], r_send.at[w, far - 1, h],
                   r_recv.at[w, far - 1, h], to)

    def reduce(k, _):
        n = z * size + k
        total = own[n] + twin[n].astype(F32)
        total = total + got[0, far - 1, k].astype(F32) + got[1, far - 1, k].astype(F32)
        shard[k] = (total / divisor[k]).astype(BF16)
        return 0

    lax.fori_loop(0, size, reduce, 0, unroll=2)

    ring = Ring(
        lambda zz, cc: amp1.at[cc, pl.ds(zz * size, size)],
        lambda zz, cc, h: amp1.at[cc, pl.ds(zz * size + h * half, half)],
        z, nz, c, lambda dz, dc: me((dz + nz) % nz, dc), sems,
    )
    @pl.when(a != z)
    def _():
        push(shard, amp2.at[z], t_send.at[0], t_recv.at[0], mirror)

    @pl.when(a == z)
    def _():
        pltpu.make_async_copy(shard, amp2.at[z], loc.at[0]).start()

    ring.start(shard, None)
    here = pltpu.make_async_copy(shard, amp1.at[c, rows(z)], loc.at[1])
    here.start()
    ring.step(0)

    @pl.when(a != z)
    def _():
        landed(amp2.at[a], t_send.at[0], t_recv.at[0], mirror)
        pltpu.make_async_remote_copy(
            src_ref=shard, dst_ref=amp2.at[z], send_sem=t_send.at[0], recv_sem=t_recv.at[0],
            device_id=mirror, device_id_type=MESH,
        ).wait_send()

    @pl.when(a == z)
    def _():
        pltpu.make_async_copy(shard, amp2.at[z], loc.at[0]).wait()

    for n, peer in enumerate(line):
        sent.append(push(amp2.at[a], amp2.at[a], x_send.at[n], x_recv.at[n], peer))
    for step in range(1, far):
        ring.step(step)
    ring.finish()
    for n, (dx, dy) in enumerate(LINE):
        fa = (x - dx + NX) % NX * 2 + (yh + dy) % 2
        landed(amp2.at[fa], x_send.at[n], x_recv.at[n], device(fa, z, c, p))
    here.wait()
    for copy in sent:
        copy.wait_send()


def amplitudes(tiles, sec, first, straight, divisor, naux, nz):
    ni, _, width = first.shape
    nb = width // BLK
    entries = ni * nb
    size = divisor.shape[0]
    block = (BLK, LANES)
    dma = pltpu.SemaphoreType.DMA
    vmem = pl.BlockSpec(memory_space=pltpu.VMEM)
    hbm = pl.BlockSpec(memory_space=pl.ANY)
    return pl.pallas_call(
        functools.partial(amplitude_kernel, naux, nz, nb),
        out_shape=[
            jax.ShapeDtypeStruct((2, entries, *block), BF16),
            jax.ShapeDtypeStruct((naux, size, *block), BF16),
        ],
        in_specs=[pl.BlockSpec(memory_space=pltpu.SMEM), hbm, hbm, vmem, vmem],
        out_specs=[hbm, hbm],
        scratch_shapes=[
            pltpu.VMEM((2, width // LANES, sec.shape[1], LANES), BF16),
            pltpu.VMEM(first.shape, BF16),
            pltpu.VMEM((entries, *block), F32),
            pltpu.VMEM((entries, *block), BF16),
            pltpu.VMEM((entries, *block), BF16),
            pltpu.VMEM((2, nz // 2, size, *block), BF16),
            pltpu.VMEM((2, nz // 2, size, *block), BF16),
            pltpu.VMEM((size, *block), BF16),
            dma((nz,)), dma((nz,)), dma((2, nz // 2, 2)), dma((2, nz // 2, 2)), dma((1,)), dma((1,)),
            dma((naux - 1,)), dma((naux - 1,)), dma((width // LANES,)), dma((3,)),
            *ring_sems(nz),
        ],
        compiler_params=pltpu.CompilerParams(
            collective_id=2, has_side_effects=True, vmem_limit_bytes=VMEM_LIMIT
        ),
        name="amplitudes",
    )(tiles, sec, first, straight, divisor)


def spread_halves(amp, b0, b1):
    lane = lax.broadcasted_iota(jnp.int32, (BLK, LANES), 1) // BLK
    turned = pltpu.roll(amp, BLK, 1)
    zero = jnp.zeros_like(amp)
    t0 = jnp.where(lane == b0 % 2, jnp.where(b0 % 2 == 0, amp, turned), zero)
    t1 = jnp.where(lane == b1 % 2, jnp.where(b1 % 2 == 1, amp, turned), zero)
    return t0, t1


class Sum:
    def __init__(self, me, up, dn, s0, r0, s1, r1):
        self.me, self.up, self.dn = me, up, dn
        self.s0, self.r0, self.s1, self.r1 = s0, r0, s1, r1

    def first(self, part, into):
        far = (self.me + 2) % 4
        return [
            push(part(far, w), into(w), self.s0.at[w], self.r0.at[w], to)
            for w, to in ((0, self.up), (1, self.dn))
        ]

    def first_landed(self, into):
        for w, to in ((0, self.dn), (1, self.up)):
            landed(into(w), self.s0.at[w], self.r0.at[w], to)

    def second(self, source, into):
        return [
            push(source(w), into(w), self.s1.at[w], self.r1.at[w], to)
            for w, to in ((0, self.up), (1, self.dn))
        ]

    def second_landed(self, into):
        for w, to in ((0, self.dn), (1, self.up)):
            landed(into(w), self.s1.at[w], self.r1.at[w], to)


def first_density_kernel(
    naux, nz, nb, tiles, sec_hbm, amp_hbm, straight, out,
    sec, amp, part, got_a, give_b, got_b, total, give_c, got_c, give_d, got_d, done,
    p1s, p1r, p2s, p2r, z_send, z_recv, s_load, loc
):
    a, z, c, p = place()
    loads = [pltpu.make_async_copy(amp_hbm, amp, loc.at[0]), *load_tiles(sec_hbm, sec, s_load)]
    for load in loads:
        load.start()
    x, y = a // 2, a % 2 * 2 + p
    frows, width = part.shape[3], part.shape[4]
    group = width // BLK
    chunk_half = width // 2

    def me(dz, dc):
        return device(a, (z + dz) % nz, (c + dc) % 2, p)

    def at_y(ty):
        return device(x * 2 + ty // 2, z, c, ty % 2)

    column = [(dz, dc) for dz in range(nz) for dc in range(2) if (dz, dc) != (0, 0)]
    right, left = device((a + 2) % naux, z, c, p), device((a + naux - 2) % naux, z, c, p)
    above, below = at_y((y + 1) % 4), at_y((y + 3) % 4)
    greet([right, left, above, below] + [me(dz, dc) for dz, dc in column])
    for load in loads:
        load.wait()
    sent = []

    def compute(k):
        chunk = (z + 1 + k) % nz

        def orbital(i, _):
            for m in range(group // 2):
                halves = []
                for e in range(2):
                    entry = chunk * group + m * 2 + e
                    rights, weights = [], []
                    for side in range(2):
                        core = c if side == 0 else 1 - c
                        at = (side * 2 + i) * nb + entry
                        rights += [sec[core, tiles[at * 2]], sec[core, tiles[at * 2 + 1]]]
                        weights += spread_masked(
                            amp[core, i * nb + entry].astype(F32), straight[pl.ds(at, 1), :] > 0.5
                        )
                    halves.append(
                        lax.dot_general(
                            jnp.concatenate(rights, axis=1),
                            jnp.concatenate(weights, axis=1).astype(BF16),
                            (((1,), (1,)), ((), ())),
                            preferred_element_type=F32,
                        )
                    )
                both = jnp.concatenate(halves, axis=1).astype(BF16)
                both = both.reshape(4, 2, frows, LANES)
                cols = slice(m * LANES, (m + 1) * LANES)
                for xx in range(4):
                    for yy in range(2):
                        u, v = (xx, yy * 2 + i) if k % 2 == 0 else (yy * 2 + i, xx)
                        part[k, u, v, :, cols] = both[xx, yy]
            return 0

        lax.fori_loop(0, 2, orbital, 0)

    def rings(k):
        over_x = (x, right, left)
        over_y = (y, above, below)
        one, two = (over_x, over_y) if k % 2 == 0 else (over_y, over_x)
        return (
            Sum(*one, p1s.at[k, 0], p1r.at[k, 0], p1s.at[k, 1], p1r.at[k, 1]),
            Sum(*two, p2s.at[k, 0], p2r.at[k, 0], p2s.at[k, 1], p2r.at[k, 1]),
        )

    def stage_b(k):
        one, _ = rings(k)
        sent.extend(
            one.first(
                lambda far, w: part.at[k, far, pl.ds(2 * w, 2)], lambda w: got_a.at[k, w]
            )
        )

    def stage_c(k):
        one, _ = rings(k)
        one.first_landed(lambda w: got_a.at[k, w])
        for w, step in ((0, 1), (1, 3)):
            u = (one.me + step) % 4
            for v in range(4):
                if v // 2 == w:
                    both = part[k, u, v].astype(F32) + got_a[k, w, v % 2].astype(F32)
                    give_b[k, w, v] = both.astype(BF16)
                else:
                    give_b[k, w, v] = part[k, u, v]
        sent.extend(one.second(lambda w: give_b.at[k, w], lambda w: got_b.at[k, w]))

    def stage_d(k):
        one, two = rings(k)
        one.second_landed(lambda w: got_b.at[k, w])
        for v in range(4):
            total[k, v] = (
                part[k, one.me, v].astype(F32)
                + got_b[k, 0, v].astype(F32) + got_b[k, 1, v].astype(F32)
            )
        far = (two.me + 2) % 4
        for w in range(2):
            give_c[k, w] = total[k, far, :, w * chunk_half:(w + 1) * chunk_half].astype(BF16)
        sent.extend(two.first(lambda far, w: give_c.at[k, w], lambda w: got_c.at[k, w]))

    def stage_e(k):
        _, two = rings(k)
        two.first_landed(lambda w: got_c.at[k, w])
        for w, step in ((0, 1), (1, 3)):
            v = (two.me + step) % 4
            for h in range(2):
                cols = slice(h * chunk_half, (h + 1) * chunk_half)
                mine = total[k, v, :, cols]
                if h == w:
                    mine = mine + got_c[k, w].astype(F32)
                give_d[k, w, :, cols] = mine.astype(BF16)
        sent.extend(two.second(lambda w: give_d.at[k, w], lambda w: got_d.at[k, w]))

    def stage_f(k):
        _, two = rings(k)
        two.second_landed(lambda w: got_d.at[k, w])
        final = total[k, two.me] + got_d[k, 0].astype(F32) + got_d[k, 1].astype(F32)
        done[k] = final.astype(BF16)
        dz = (k + 1) % nz
        for dc in range(2):
            cc = (c + dc) % 2
            source = done.at[k, :, pl.ds(pl.multiple_of(cc * chunk_half, chunk_half), chunk_half)]
            if (dz, dc) == (0, 0):
                pltpu.make_async_copy(source, out.at[z * 2 + c], loc.at[1]).start()
            else:
                n = dz * 2 + dc
                sent.append(
                    push(source, out.at[z * 2 + c], z_send.at[n], z_recv.at[n], me(dz, dc))
                )

    stages = (stage_b, stage_c, stage_d, stage_e, stage_f)
    for k in range(nz + len(stages) - 1):
        if k < nz:
            compute(k)
        for lag, stage in enumerate(stages):
            if 0 <= k - lag < nz:
                stage(k - lag)

    for dz, dc in column:
        fz, fc = (z - dz + nz) % nz, (c + dc) % 2
        n = dz * 2 + dc
        landed(out.at[fz * 2 + fc], z_send.at[n], z_recv.at[n], device(a, fz, fc, p))
    pltpu.make_async_copy(
        done.at[nz - 1, :, pl.ds(pl.multiple_of(c * chunk_half, chunk_half), chunk_half)],
        out.at[z * 2 + c], loc.at[1],
    ).wait()
    for copy in sent:
        copy.wait_send()


def first_density_of(tiles, sec, amp, straight, naux, nz):
    _, rows, width = sec.shape
    nb = width // BLK
    frows, chunk = rows // naux, width // nz
    dma = pltpu.SemaphoreType.DMA
    hbm = pl.BlockSpec(memory_space=pl.ANY)
    return pl.pallas_call(
        functools.partial(first_density_kernel, naux, nz, nb),
        out_shape=jax.ShapeDtypeStruct((nz * 2, frows, chunk // 2), BF16),
        in_specs=[
            pl.BlockSpec(memory_space=pltpu.SMEM), hbm, hbm, pl.BlockSpec(memory_space=pltpu.VMEM)
        ],
        out_specs=hbm,
        scratch_shapes=[
            pltpu.VMEM((2, width // LANES, rows, LANES), BF16),
            pltpu.VMEM(amp.shape, BF16),
            pltpu.VMEM((nz, 4, 4, frows, chunk), BF16),
            pltpu.VMEM((nz, 2, 2, frows, chunk), BF16),
            pltpu.VMEM((nz, 2, 4, frows, chunk), BF16),
            pltpu.VMEM((nz, 2, 4, frows, chunk), BF16),
            pltpu.VMEM((nz, 4, frows, chunk), F32),
            pltpu.VMEM((nz, 2, frows, chunk // 2), BF16),
            pltpu.VMEM((nz, 2, frows, chunk // 2), BF16),
            pltpu.VMEM((nz, 2, frows, chunk), BF16),
            pltpu.VMEM((nz, 2, frows, chunk), BF16),
            pltpu.VMEM((nz, frows, chunk), BF16),
            dma((nz, 2, 2)), dma((nz, 2, 2)), dma((nz, 2, 2)), dma((nz, 2, 2)),
            dma((nz * 2,)), dma((nz * 2,)), dma((width // LANES,)), dma((2,)),
        ],
        compiler_params=pltpu.CompilerParams(
            collective_id=3, has_side_effects=True, vmem_limit_bytes=VMEM_LIMIT
        ),
        name="first_density",
    )(tiles, sec, amp, straight)


def toward_second_kernel(group, nb, kept, first, amp, out, total):
    i, g = pl.program_id(0), pl.program_id(1)

    @pl.when((i == 0) & (g == 0))
    def _():
        total[...] = jnp.zeros_like(total)

    nothing = jnp.zeros((BLK, 2 * LANES), BF16)
    for pairs in range(group // 2):
        left = first[0, :, pairs * LANES:(pairs + 1) * LANES]
        for e in range(2):
            entry = pairs * 2 + e
            at = (i * nb + g * group + entry) * 2
            b0, b1 = kept[at], kept[at + 1]
            t0, t1 = spread_halves(amp[entry].astype(F32), b0, b1)
            weights = jnp.concatenate([t0, t1], axis=1).astype(BF16)
            stack = [weights, nothing] if e == 0 else [nothing, weights]
            term = jnp.dot(left, jnp.concatenate(stack, axis=0), preferred_element_type=F32)
            for b, part in ((b0, term[:, :LANES]), (b1, term[:, LANES:])):
                at_lanes = pl.ds(pl.multiple_of(b // 2 * LANES, LANES), LANES)
                total[:, at_lanes] += part

    @pl.when((i == pl.num_programs(0) - 1) & (g == pl.num_programs(1) - 1))
    def _():
        out[...] = total[...].astype(BF16)


def toward_second(kept, first, amp, group=8):
    ni, rows, width = first.shape
    nb = width // BLK
    groups = nb // group
    return pl.pallas_call(
        functools.partial(toward_second_kernel, group, nb),
        out_shape=jax.ShapeDtypeStruct((rows, width), BF16),
        grid_spec=pltpu.PrefetchScalarGridSpec(
            num_scalar_prefetch=1,
            grid=(ni, groups),
            in_specs=[
                pl.BlockSpec((1, rows, group * BLK), lambda i, g, kept: (i, 0, g)),
                pl.BlockSpec((group, BLK, LANES), lambda i, g, kept: (i * groups + g, 0, 0)),
            ],
            out_specs=pl.BlockSpec((rows, width), lambda i, g, kept: (0, 0)),
            scratch_shapes=[pltpu.VMEM((rows, width), F32)],
        ),
        compiler_params=pltpu.CompilerParams(vmem_limit_bytes=VMEM_LIMIT),
        name="toward_second",
    )(kept, first, amp)


def shards(first_factors, second_factors, first_energy, second_energy, virtual_energy, kept_blocks):
    naux, nz = lax.axis_size("aux"), lax.axis_size("occ") // 2
    a, z, c, p = place()
    rows, nj, width = second_factors.shape
    frows, ni, _ = first_factors.shape
    nb = width // BLK
    entries = ni * nb

    order = [
        (aa * 2 * nz + zz * 2 + cc, zz * 2 * nz + aa * 2 + cc)
        for aa in range(naux) for zz in range(nz) for cc in range(2)
    ]
    kept_here = kept_blocks[:, 0].reshape(entries * 2)
    kept_mine = lax.ppermute(kept_here, ("aux", "occ"), order)
    energy_mine = lax.ppermute(second_energy, ("aux", "occ"), order)
    swap = [(o, o // 2 * 2 + 1 - o % 2) for o in range(2 * nz)]
    kept_twin = lax.ppermute(kept_mine, "occ", swap)
    kept = jnp.concatenate([kept_mine, kept_twin])
    tiles = kept // 2
    in_place = jnp.stack([kept[0::2] % 2 == 0, kept[1::2] % 2 == 1], axis=1)
    straight = jnp.repeat(in_place.astype(F32), BLK, axis=1)

    size = entries // nz
    energy_blocks = virtual_energy.reshape(nb, BLK)
    picked = lax.dynamic_slice_in_dim(kept_mine, z * size * 2, size * 2, 0)
    entry = z * size + jnp.arange(size)
    left = jnp.take(energy_blocks, entry % nb, axis=0)
    right = jnp.take(energy_blocks, picked, axis=0).reshape(size, 2 * BLK)
    low = jnp.take(first_energy, entry // nb)
    divisor = left[:, :, None] + right[:, None, :] - low[:, None, None] - energy_mine[0]

    second = jnp.transpose(second_factors, (1, 0, 2)).reshape(naux, 2, 2, rows, width)
    first = jnp.transpose(first_factors, (1, 0, 2))
    sec, firstz, firsta = spread(second, first, naux, nz)
    sec = sec.reshape(2, naux * 2 * rows, width)
    firstz = firstz.reshape(ni, naux * frows, width)
    firsta = firsta.reshape(ni, nz * 2 * frows, width)

    amp1, amp2 = amplitudes(tiles, sec, firstz, straight, divisor, naux, nz)
    first_density = first_density_of(tiles, sec, amp1, straight, naux, nz)
    amp2 = amp2.reshape(entries, BLK, LANES)
    second_density = toward_second(kept_here, firsta, amp2)
    return (
        first_density.reshape(nz * 2 * frows, 1, width // (nz * 2)),
        second_density.reshape(nz * 2 * frows, 1, width),
    )


def solution(mesh):
    placed = (
        P(("aux", "occ"), None, None),
        P(("aux", "occ", "pair"), None, None),
        P(),
        P(("occ", "pair")),
        P(),
        P(None, ("occ", "pair"), None, None),
    )
    return jax.shard_map(
        shards,
        mesh=mesh,
        in_specs=placed,
        out_specs=(P("aux", "pair", "occ"), P("aux", ("occ", "pair"), None)),
        check_vma=False,
    )
```

```python
import functools

import jax
import jax.numpy as jnp
from jax import lax
from jax.experimental import pallas as pl
from jax.experimental.pallas import tpu as pltpu
from jax.sharding import PartitionSpec as P

MESH = pl.DeviceIdType.MESH
F32 = jnp.float32
BF16 = jnp.bfloat16
BLK = 64
LANES = 128
NX = 4
ORDER = (
    (1, 0), (0, 1), (3, 0), (0, 3), (1, 1), (3, 3), (1, 3), (3, 1),
    (2, 0), (0, 2), (2, 1), (1, 2), (2, 3), (3, 2), (2, 2),
)
LINE = ((1, 0), (3, 0), (0, 1), (2, 0), (1, 1), (3, 1), (2, 1))
VMEM_LIMIT = 52 * 1024 * 1024


def place():
    aux, occ, pair = lax.axis_index("aux"), lax.axis_index("occ"), lax.axis_index("pair")
    return aux, occ // 2, occ % 2, pair


def device(aux, z, core, pair):
    return {"aux": aux, "occ": z * 2 + core, "pair": pair}


def push(src, dst, send, recv, to):
    copy = pltpu.make_async_remote_copy(
        src_ref=src, dst_ref=dst, send_sem=send, recv_sem=recv, device_id=to, device_id_type=MESH
    )
    copy.start()
    return copy


def landed(ref, send, recv, to):
    pltpu.make_async_remote_copy(
        src_ref=ref, dst_ref=ref, send_sem=send, recv_sem=recv, device_id=to, device_id_type=MESH
    ).wait_recv()


def greet(peers):
    barrier = pltpu.get_barrier_semaphore()
    for peer in peers:
        pl.semaphore_signal(barrier, inc=1, device_id=peer, device_id_type=MESH)
    pl.semaphore_wait(barrier, len(peers))


def plane_peers(a, z, c, p, naux):
    return [
        device((a + da) % naux, z, c, (p + dp) % 2)
        for da in range(naux)
        for dp in range(2)
        if (da, dp) != (0, 0)
    ]


class Ring:
    def __init__(self, block, half, z, nz, c, me, sems):
        self.block, self.half, self.z, self.nz, self.c = block, half, z, nz, c
        self.me = me
        self.up_send, self.up_recv, self.dn_send, self.dn_recv, self.co_send, self.co_recv = sems
        self.up, self.dn, self.co = me(1, 0), me(-1, 0), me(0, 1)
        self.far = nz // 2
        self.sent = []

    def piece(self, way, step, core):
        origin = (self.z - way * (step + 1) + self.nz) % self.nz
        if step + 1 == self.far:
            return self.half(origin, core, 0 if way > 0 else 1)
        return self.block(origin, core)

    def start(self, source, source_halves):
        mine = self.block(self.z, self.c)
        if self.far == 1:
            raise ValueError("short ring")
        self.sent.append(push(source, mine, self.up_send.at[0], self.up_recv.at[0], self.up))
        self.sent.append(push(source, mine, self.dn_send.at[0], self.dn_recv.at[0], self.dn))
        self.sent.append(push(source, mine, self.co_send.at[0], self.co_recv.at[0], self.co))

    def step(self, step):
        for way, send, recv, to in (
            (1, self.up_send, self.up_recv, self.up),
            (-1, self.dn_send, self.dn_recv, self.dn),
        ):
            got = self.piece(way, step, self.c)
            landed(got, send.at[step], recv.at[step], to)
            if step + 1 < self.far:
                onward = got
                if step + 2 == self.far:
                    origin = (self.z - way * (step + 1) + self.nz) % self.nz
                    onward = self.half(origin, self.c, 0 if way > 0 else 1)
                self.sent.append(push(onward, onward, send.at[step + 1], recv.at[step + 1], to))
            k = 1 + 2 * step + (0 if way > 0 else 1)
            self.sent.append(push(got, got, self.co_send.at[k], self.co_recv.at[k], self.co))

    def finish(self):
        other = 1 - self.c
        landed(self.block(self.z, other), self.co_send.at[0], self.co_recv.at[0], self.co)
        for step in range(self.far):
            for way in (1, -1):
                k = 1 + 2 * step + (0 if way > 0 else 1)
                landed(self.piece(way, step, other), self.co_send.at[k], self.co_recv.at[k], self.co)
        for copy in self.sent:
            copy.wait_send()


def ring_sems(nz):
    far = nz // 2
    return [pltpu.SemaphoreType.DMA((far,))] * 4 + [pltpu.SemaphoreType.DMA((1 + 2 * far,))] * 2


def spread_kernel(
    naux, nz, second, first, sec, firstz, firsta, a_send, a_recv, b_send, b_recv, loc, *sems
):
    a, z, c, p = place()
    x, yh = a // 2, a % 2

    def me(dz, dc):
        return device(a, (z + dz + nz) % nz, (c + dc) % 2, p)

    in_plane = plane_peers(a, z, c, p, naux)
    greet(in_plane + [me(1, 0), me(-1, 0), me(0, 1)])

    locals_ = [
        pltpu.make_async_copy(first, firstz.at[:, a], loc.at[0]),
        pltpu.make_async_copy(first, firsta.at[:, z * 2 + c], loc.at[1]),
        pltpu.make_async_copy(second.at[a, :, p], sec.at[:, a * 2 + p], loc.at[2]),
    ]
    sent = []
    right = device((x + 1) % NX * 2 + yh, z, c, p)
    left = device((x + NX - 1) % NX * 2 + yh, z, c, p)
    across = device(x * 2 + (1 - yh), z, c, 1 - p)
    beside = device(a, z, c, 1 - p)
    al = (x + NX - 1) % NX * 2 + yh
    ar = (x + 1) % NX * 2 + yh
    af = (x + 2) % NX * 2 + yh
    sent.append(push(first, firstz.at[:, a], b_send.at[0], b_recv.at[0], right))
    sent.append(push(first, firstz.at[:, a], b_send.at[1], b_recv.at[1], left))
    sent.append(push(first.at[p], firstz.at[p, a], b_send.at[4], b_recv.at[4], across))
    ring = Ring(
        lambda zz, cc: firsta.at[:, zz * 2 + cc],
        lambda zz, cc, h: firsta.at[h, zz * 2 + cc],
        z, nz, c, me, sems,
    )
    ring.start(first, None)
    y = yh * 2 + p
    batches = [4, 2, 2, 2, 2, 2, 1]

    def plane(dx, dy):
        ty = (y + dy) % 4
        return (x + dx) % NX * 2 + ty // 2, ty % 2

    def send_some():
        for _ in range(batches.pop(0) if batches else 0):
            n = len(second_sent)
            ta, tp = plane(*ORDER[n])
            second_sent.append(
                push(second.at[ta, :, tp], sec.at[:, a * 2 + p], a_send.at[n], a_recv.at[n],
                     device(ta, z, c, tp))
            )

    second_sent = []
    send_some()
    for copy in locals_:
        copy.start()

    landed(firstz.at[:, al], b_send.at[0], b_recv.at[0], left)
    sent.append(push(firstz.at[0, al], firstz.at[0, al], b_send.at[2], b_recv.at[2], right))
    sent.append(push(firstz.at[p, al], firstz.at[p, al], b_send.at[5], b_recv.at[5], across))
    send_some()
    landed(firstz.at[:, ar], b_send.at[1], b_recv.at[1], right)
    sent.append(push(firstz.at[1, ar], firstz.at[1, ar], b_send.at[3], b_recv.at[3], left))
    sent.append(push(firstz.at[p, ar], firstz.at[p, ar], b_send.at[6], b_recv.at[6], across))
    send_some()
    ring.step(0)
    send_some()

    def relay(k, slot):
        got = firstz.at[1 - p, slot // 2 * 2 + (1 - yh)]
        landed(got, b_send.at[4 + k], b_recv.at[4 + k], across)
        sent.append(push(got, got, b_send.at[8 + k], b_recv.at[8 + k], beside))

    relay(0, a)
    send_some()
    landed(firstz.at[0, af], b_send.at[2], b_recv.at[2], left)
    landed(firstz.at[1, af], b_send.at[3], b_recv.at[3], right)
    sent.append(push(firstz.at[p, af], firstz.at[p, af], b_send.at[7], b_recv.at[7], across))
    send_some()
    ring.step(1)
    send_some()
    relay(1, al)
    relay(2, ar)
    ring.step(2)
    relay(3, af)
    ring.step(3)
    for k, slot in enumerate((a, al, ar, af)):
        got = firstz.at[p, slot // 2 * 2 + (1 - yh)]
        landed(got, b_send.at[8 + k], b_recv.at[8 + k], beside)
    ring.finish()
    for n, (dx, dy) in enumerate(ORDER):
        fa, fp = plane(NX - dx, 4 - dy)
        landed(sec.at[:, fa * 2 + fp], a_send.at[n], a_recv.at[n], device(fa, z, c, fp))
    for copy in second_sent:
        copy.wait_send()
    for copy in sent:
        copy.wait_send()
    for copy in locals_:
        copy.wait()


def spread(second, first, naux, nz):
    _, _, _, rows, width = second.shape
    ni, frows, _ = first.shape
    return pl.pallas_call(
        functools.partial(spread_kernel, naux, nz),
        out_shape=[
            jax.ShapeDtypeStruct((2, naux * 2, rows, width), BF16),
            jax.ShapeDtypeStruct((ni, naux, frows, width), BF16),
            jax.ShapeDtypeStruct((ni, nz * 2, frows, width), BF16),
        ],
        in_specs=[pl.BlockSpec(memory_space=pl.ANY)] * 2,
        out_specs=[pl.BlockSpec(memory_space=pl.ANY)] * 3,
        scratch_shapes=[
            pltpu.SemaphoreType.DMA((naux * 2 - 1,)),
            pltpu.SemaphoreType.DMA((naux * 2 - 1,)),
            pltpu.SemaphoreType.DMA((12,)),
            pltpu.SemaphoreType.DMA((12,)),
            pltpu.SemaphoreType.DMA((3,)),
            *ring_sems(nz),
        ],
        compiler_params=pltpu.CompilerParams(
            collective_id=1, has_side_effects=True, vmem_limit_bytes=VMEM_LIMIT
        ),
        name="spread",
    )(second, first)


def load_tiles(sec_hbm, sec, sem):
    return [
        pltpu.make_async_copy(sec_hbm.at[:, :, pl.ds(t * LANES, LANES)], sec.at[:, t], sem.at[t])
        for t in range(sec.shape[1])
    ]


def spread_masked(amp, straight):
    lane = lax.broadcasted_iota(jnp.int32, (BLK, LANES), 1)
    zero = jnp.zeros_like(amp)
    stay = jnp.where(straight, amp, zero)
    move = pltpu.roll(jnp.where(straight, zero, amp), BLK, 1)
    return jnp.where(lane < BLK, stay, move), jnp.where(lane < BLK, move, stay)


def amplitude_kernel(
    naux, nz, nb, tiles, sec_hbm, first_hbm, straight, divisor, amp, mine,
    sec, first, own, other, twin, outgoing, got, shard,
    d_send, d_recv, r_send, r_recv, t_send, t_recv, s_load, loc, *sems
):
    a, z, c, p = place()
    size = divisor.shape[0]
    loads = [pltpu.make_async_copy(first_hbm, first, loc.at[0]), *load_tiles(sec_hbm, sec, s_load)]
    for load in loads:
        load.start()
    far, half = nz // 2, size // 2

    def me(dz, dc):
        return device(a, (z + dz) % nz, (c + dc) % 2, p)

    sibling = me(0, 1)
    line = [device((a + da) % naux, z, c, p) for da in range(1, naux)]
    greet([sibling, me(1, 0), me(nz - 1, 0)] + line)
    for load in loads:
        load.wait()
    lane = lax.broadcasted_iota(jnp.int32, (BLK, LANES), 1)

    def rows(t):
        return pl.ds(t * size, size)

    sent = []

    def compute(dz):
        t = (z + dz) % nz
        i, start = t * size // nb, t * size % nb

        def two(k, _):
            tile = pl.ds(pl.multiple_of((start // 2 + k) * LANES, LANES), LANES)
            left = first[i, :, tile].T
            for side, out in ((0, own), (1, other)):
                which = c if side == 0 else 1 - c
                for e in range(2):
                    at = (side * 2 + i) * nb + start + k * 2 + e
                    right = jnp.concatenate(
                        [sec[which, tiles[at * 2]], sec[which, tiles[at * 2 + 1]]], axis=1
                    )
                    prod = lax.dot_general(
                        left[e * BLK:(e + 1) * BLK], right, (((1,), (0,)), ((), ())),
                        preferred_element_type=F32,
                    )
                    u0, u1 = prod[:, :LANES], prod[:, LANES:]
                    stay = jnp.where(lane < BLK, u0, u1)
                    move = pltpu.roll(jnp.where(lane < BLK, u1, u0), BLK, 1)
                    chosen = jnp.where(straight[pl.ds(at, 1), :] > 0.5, stay, move)
                    out[t * size + k * 2 + e] = chosen.astype(out.dtype)
            return 0

        lax.fori_loop(0, size // 2, two, 0)
        sent.append(
            push(other.at[rows(t)], twin.at[rows(t)], d_send.at[dz], d_recv.at[dz], sibling)
        )

    ways = ((1, 0, me(1, 0)), (-1, 1, me(nz - 1, 0)))

    def reduce_step(step, way, w, to):
        dz = way * (far - step) % nz
        t = (z + dz) % nz
        if step or w == 0:
            landed(twin.at[rows(t)], d_send.at[dz], d_recv.at[dz], sibling)

        def add(k, _):
            n = t * size + k
            total = own[n] + twin[n].astype(F32)
            outgoing[w, step, k] = total.astype(BF16)
            return 0

        def add_got(k, _):
            n = t * size + k
            total = own[n] + twin[n].astype(F32) + got[w, step - 1, k].astype(F32)
            outgoing[w, step, k] = total.astype(BF16)
            return 0

        for h in (1 - w, w):
            if step == 0 and h != w:
                continue
            span = pl.ds(h * half, half)
            if step > 1 or (step == 1 and h == w):
                landed(got.at[w, step - 1, span], r_send.at[w, step - 1, h],
                       r_recv.at[w, step - 1, h], to)
                lax.fori_loop(h * half, h * half + half, add_got, 0, unroll=4)
            else:
                lax.fori_loop(h * half, h * half + half, add, 0, unroll=4)
            sent.append(
                push(outgoing.at[w, step, span], got.at[w, step, span],
                     r_send.at[w, step, h], r_recv.at[w, step, h], to)
            )

    compute(far)
    compute(far - 1)
    reduce_step(0, *ways[0])
    reduce_step(0, *ways[1])
    for step in range(1, far):
        compute(nz - far + step)
        reduce_step(step, *ways[0])
        compute(far - 1 - step)
        reduce_step(step, *ways[1])

    landed(twin.at[rows(z)], d_send.at[0], d_recv.at[0], sibling)
    for way, w, to in ways:
        for h in range(2):
            landed(got.at[w, far - 1, pl.ds(h * half, half)], r_send.at[w, far - 1, h],
                   r_recv.at[w, far - 1, h], to)

    def reduce(k, _):
        n = z * size + k
        total = own[n] + twin[n].astype(F32)
        total = total + got[0, far - 1, k].astype(F32) + got[1, far - 1, k].astype(F32)
        shard[k] = (total / divisor[k]).astype(BF16)
        return 0

    lax.fori_loop(0, size, reduce, 0, unroll=2)

    ring = Ring(
        lambda zz, cc: amp.at[cc, pl.ds(zz * size, size)],
        lambda zz, cc, h: amp.at[cc, pl.ds(zz * size + h * half, half)],
        z, nz, c, lambda dz, dc: me((dz + nz) % nz, dc), sems,
    )
    ring.start(shard, None)
    here = pltpu.make_async_copy(shard, amp.at[c, rows(z)], loc.at[1])
    here.start()

    keep = pltpu.make_async_copy(shard, mine, loc.at[2])

    @pl.when(a == z)
    def _():
        keep.start()

    def hand_out(n, start):
        s = (z + n) % nz
        copy = pltpu.make_async_remote_copy(
            src_ref=amp.at[c, rows(s)], dst_ref=mine, send_sem=t_send.at[n - 1],
            recv_sem=t_recv.at[0], device_id=device(s, z, c, p), device_id_type=MESH,
        )
        if start:
            copy.start()
        else:
            copy.wait_send()

    for step in range(far):
        ring.step(step)

        @pl.when(a == z)
        def _():
            for n in sorted({step + 1, nz - 1 - step}):
                hand_out(n, True)

    ring.finish()

    @pl.when(a == z)
    def _():
        keep.wait()
        for n in range(1, nz):
            hand_out(n, False)

    @pl.when(a != z)
    def _():
        landed(mine, t_send.at[0], t_recv.at[0], device(z, z, c, p))

    here.wait()
    for copy in sent:
        copy.wait_send()


def amplitudes(tiles, sec, first, straight, divisor, naux, nz):
    ni, _, width = first.shape
    nb = width // BLK
    entries = ni * nb
    size = divisor.shape[0]
    block = (BLK, LANES)
    dma = pltpu.SemaphoreType.DMA
    vmem = pl.BlockSpec(memory_space=pltpu.VMEM)
    hbm = pl.BlockSpec(memory_space=pl.ANY)
    return pl.pallas_call(
        functools.partial(amplitude_kernel, naux, nz, nb),
        out_shape=[
            jax.ShapeDtypeStruct((2, entries, *block), BF16),
            jax.ShapeDtypeStruct((size, *block), BF16),
        ],
        in_specs=[pl.BlockSpec(memory_space=pltpu.SMEM), hbm, hbm, vmem, vmem],
        out_specs=[hbm, hbm],
        scratch_shapes=[
            pltpu.VMEM((2, width // LANES, sec.shape[1], LANES), BF16),
            pltpu.VMEM(first.shape, BF16),
            pltpu.VMEM((entries, *block), F32),
            pltpu.VMEM((entries, *block), BF16),
            pltpu.VMEM((entries, *block), BF16),
            pltpu.VMEM((2, nz // 2, size, *block), BF16),
            pltpu.VMEM((2, nz // 2, size, *block), BF16),
            pltpu.VMEM((size, *block), BF16),
            dma((nz,)), dma((nz,)), dma((2, nz // 2, 2)), dma((2, nz // 2, 2)),
            dma((nz - 1,)), dma((1,)), dma((width // LANES,)), dma((3,)),
            *ring_sems(nz),
        ],
        compiler_params=pltpu.CompilerParams(
            collective_id=2, has_side_effects=True, vmem_limit_bytes=VMEM_LIMIT
        ),
        name="amplitudes",
    )(tiles, sec, first, straight, divisor)


class Sum:
    def __init__(self, me, up, dn, s0, r0, s1, r1):
        self.me, self.up, self.dn = me, up, dn
        self.s0, self.r0, self.s1, self.r1 = s0, r0, s1, r1

    def first(self, part, into):
        far = (self.me + 2) % 4
        return [
            push(part(far, w), into(w), self.s0.at[w], self.r0.at[w], to)
            for w, to in ((0, self.up), (1, self.dn))
        ]

    def first_landed(self, into):
        for w, to in ((0, self.dn), (1, self.up)):
            landed(into(w), self.s0.at[w], self.r0.at[w], to)

    def second(self, source, into):
        return [
            push(source(w), into(w), self.s1.at[w], self.r1.at[w], to)
            for w, to in ((0, self.up), (1, self.dn))
        ]

    def second_landed(self, into):
        for w, to in ((0, self.dn), (1, self.up)):
            landed(into(w), self.s1.at[w], self.r1.at[w], to)


def first_density_kernel(
    naux, nz, nb, tiles, sec_hbm, amp_hbm, mine, straight, out, amps,
    sec, amp, part, got_a, give_b, got_b, total, give_c, got_c, give_d, got_d, done,
    p1s, p1r, p2s, p2r, z_send, z_recv, x_send, x_recv, s_load, loc
):
    a, z, c, p = place()
    loads = [pltpu.make_async_copy(amp_hbm, amp, loc.at[0]), *load_tiles(sec_hbm, sec, s_load)]
    for load in loads:
        load.start()
    x, y = a // 2, a % 2 * 2 + p
    frows, width = part.shape[3], part.shape[4]
    group = width // BLK
    chunk_half = width // 2

    def me(dz, dc):
        return device(a, (z + dz) % nz, (c + dc) % 2, p)

    def at_y(ty):
        return device(x * 2 + ty // 2, z, c, ty % 2)

    column = [(dz, dc) for dz in range(nz) for dc in range(2) if (dz, dc) != (0, 0)]
    right, left = device((a + 2) % naux, z, c, p), device((a + naux - 2) % naux, z, c, p)
    above, below = at_y((y + 1) % 4), at_y((y + 3) % 4)
    yh = a % 2
    line = [device((x + dx) % NX * 2 + (yh + dy) % 2, z, c, p) for dx, dy in LINE]
    greet(line + [above, below] + [me(dz, dc) for dz, dc in column])
    keep = pltpu.make_async_copy(mine, amps.at[a], loc.at[2])
    keep.start()
    for load in loads:
        load.wait()
    sent = []

    def pass_on(n):
        sent.append(push(mine, amps.at[a], x_send.at[n], x_recv.at[n], line[n]))

    def compute(k):
        chunk = (z + 1 + k) % nz

        def orbital(i, _):
            for m in range(group // 2):
                halves = []
                for e in range(2):
                    entry = chunk * group + m * 2 + e
                    rights, weights = [], []
                    for side in range(2):
                        core = c if side == 0 else 1 - c
                        at = (side * 2 + i) * nb + entry
                        rights += [sec[core, tiles[at * 2]], sec[core, tiles[at * 2 + 1]]]
                        weights += spread_masked(
                            amp[core, i * nb + entry].astype(F32), straight[pl.ds(at, 1), :] > 0.5
                        )
                    halves.append(
                        lax.dot_general(
                            jnp.concatenate(rights, axis=1),
                            jnp.concatenate(weights, axis=1).astype(BF16),
                            (((1,), (1,)), ((), ())),
                            preferred_element_type=F32,
                        )
                    )
                both = jnp.concatenate(halves, axis=1).astype(BF16)
                both = both.reshape(4, 2, frows, LANES)
                cols = slice(m * LANES, (m + 1) * LANES)
                for xx in range(4):
                    for yy in range(2):
                        u, v = (xx, yy * 2 + i) if k % 2 == 0 else (yy * 2 + i, xx)
                        part[k, u, v, :, cols] = both[xx, yy]
            return 0

        lax.fori_loop(0, 2, orbital, 0)

    def rings(k):
        over_x = (x, right, left)
        over_y = (y, above, below)
        one, two = (over_x, over_y) if k % 2 == 0 else (over_y, over_x)
        return (
            Sum(*one, p1s.at[k, 0], p1r.at[k, 0], p1s.at[k, 1], p1r.at[k, 1]),
            Sum(*two, p2s.at[k, 0], p2r.at[k, 0], p2s.at[k, 1], p2r.at[k, 1]),
        )

    def stage_b(k):
        one, _ = rings(k)
        sent.extend(
            one.first(
                lambda far, w: part.at[k, far, pl.ds(2 * w, 2)], lambda w: got_a.at[k, w]
            )
        )

    def stage_c(k):
        one, _ = rings(k)
        one.first_landed(lambda w: got_a.at[k, w])
        for w, step in ((0, 1), (1, 3)):
            u = (one.me + step) % 4
            for v in range(4):
                if v // 2 == w:
                    both = part[k, u, v].astype(F32) + got_a[k, w, v % 2].astype(F32)
                    give_b[k, w, v] = both.astype(BF16)
                else:
                    give_b[k, w, v] = part[k, u, v]
        sent.extend(one.second(lambda w: give_b.at[k, w], lambda w: got_b.at[k, w]))

    def stage_d(k):
        one, two = rings(k)
        one.second_landed(lambda w: got_b.at[k, w])
        for v in range(4):
            total[k, v] = (
                part[k, one.me, v].astype(F32)
                + got_b[k, 0, v].astype(F32) + got_b[k, 1, v].astype(F32)
            )
        far = (two.me + 2) % 4
        for w in range(2):
            give_c[k, w] = total[k, far, :, w * chunk_half:(w + 1) * chunk_half].astype(BF16)
        sent.extend(two.first(lambda far, w: give_c.at[k, w], lambda w: got_c.at[k, w]))

    def stage_e(k):
        _, two = rings(k)
        two.first_landed(lambda w: got_c.at[k, w])
        for w, step in ((0, 1), (1, 3)):
            v = (two.me + step) % 4
            for h in range(2):
                cols = slice(h * chunk_half, (h + 1) * chunk_half)
                mine = total[k, v, :, cols]
                if h == w:
                    mine = mine + got_c[k, w].astype(F32)
                give_d[k, w, :, cols] = mine.astype(BF16)
        sent.extend(two.second(lambda w: give_d.at[k, w], lambda w: got_d.at[k, w]))

    def stage_f(k):
        _, two = rings(k)
        two.second_landed(lambda w: got_d.at[k, w])
        final = total[k, two.me] + got_d[k, 0].astype(F32) + got_d[k, 1].astype(F32)
        done[k] = final.astype(BF16)
        dz = (k + 1) % nz
        for dc in range(2):
            cc = (c + dc) % 2
            source = done.at[k, :, pl.ds(pl.multiple_of(cc * chunk_half, chunk_half), chunk_half)]
            if (dz, dc) == (0, 0):
                pltpu.make_async_copy(source, out.at[z * 2 + c], loc.at[1]).start()
            else:
                n = dz * 2 + dc
                sent.append(
                    push(source, out.at[z * 2 + c], z_send.at[n], z_recv.at[n], me(dz, dc))
                )

    stages = ((stage_b, 0), (stage_c, 2), (stage_d, 5), (stage_e, 7), (stage_f, 9))
    waiting = list(range(len(line)))
    for k in range(nz + stages[-1][1]):
        if k < nz:
            compute(k)
        for stage, lag in stages:
            if 0 <= k - lag < nz:
                stage(k - lag)
        if waiting:
            pass_on(waiting.pop(0))

    for dz, dc in column:
        fz, fc = (z - dz + nz) % nz, (c + dc) % 2
        n = dz * 2 + dc
        landed(out.at[fz * 2 + fc], z_send.at[n], z_recv.at[n], device(a, fz, fc, p))
    pltpu.make_async_copy(
        done.at[nz - 1, :, pl.ds(pl.multiple_of(c * chunk_half, chunk_half), chunk_half)],
        out.at[z * 2 + c], loc.at[1],
    ).wait()
    keep.wait()
    for n, (dx, dy) in enumerate(LINE):
        fa = (x - dx + NX) % NX * 2 + (yh + dy) % 2
        landed(amps.at[fa], x_send.at[n], x_recv.at[n], device(fa, z, c, p))
    for copy in sent:
        copy.wait_send()


def first_density_of(tiles, sec, amp, mine, straight, naux, nz):
    _, rows, width = sec.shape
    nb = width // BLK
    frows, chunk = rows // naux, width // nz
    dma = pltpu.SemaphoreType.DMA
    hbm = pl.BlockSpec(memory_space=pl.ANY)
    return pl.pallas_call(
        functools.partial(first_density_kernel, naux, nz, nb),
        out_shape=[
            jax.ShapeDtypeStruct((nz * 2, frows, chunk // 2), BF16),
            jax.ShapeDtypeStruct((naux, *mine.shape), BF16),
        ],
        in_specs=[
            pl.BlockSpec(memory_space=pltpu.SMEM), hbm, hbm, hbm,
            pl.BlockSpec(memory_space=pltpu.VMEM),
        ],
        out_specs=[hbm, hbm],
        scratch_shapes=[
            pltpu.VMEM((2, width // LANES, rows, LANES), BF16),
            pltpu.VMEM(amp.shape, BF16),
            pltpu.VMEM((nz, 4, 4, frows, chunk), BF16),
            pltpu.VMEM((nz, 2, 2, frows, chunk), BF16),
            pltpu.VMEM((nz, 2, 4, frows, chunk), BF16),
            pltpu.VMEM((nz, 2, 4, frows, chunk), BF16),
            pltpu.VMEM((nz, 4, frows, chunk), F32),
            pltpu.VMEM((nz, 2, frows, chunk // 2), BF16),
            pltpu.VMEM((nz, 2, frows, chunk // 2), BF16),
            pltpu.VMEM((nz, 2, frows, chunk), BF16),
            pltpu.VMEM((nz, 2, frows, chunk), BF16),
            pltpu.VMEM((nz, frows, chunk), BF16),
            dma((nz, 2, 2)), dma((nz, 2, 2)), dma((nz, 2, 2)), dma((nz, 2, 2)),
            dma((nz * 2,)), dma((nz * 2,)), dma((naux - 1,)), dma((naux - 1,)),
            dma((width // LANES,)), dma((3,)),
        ],
        compiler_params=pltpu.CompilerParams(
            collective_id=3, has_side_effects=True, vmem_limit_bytes=VMEM_LIMIT
        ),
        name="first_density",
    )(tiles, sec, amp, mine, straight)


def toward_second_kernel(group, nb, kept, first, amp, out, total):
    i, g = pl.program_id(0), pl.program_id(1)

    @pl.when((i == 0) & (g == 0))
    def _():
        total[...] = jnp.zeros_like(total)

    lane = lax.broadcasted_iota(jnp.int32, (LANES, LANES), 1)
    for pairs in range(group // 2):
        left = first[0, :, pairs * LANES:(pairs + 1) * LANES]
        turned = jnp.concatenate(
            [amp[pairs * 2].astype(F32), amp[pairs * 2 + 1].astype(F32)], axis=0
        ).T
        zero = jnp.zeros_like(turned)
        weights = jnp.concatenate(
            [jnp.where(lane < BLK, turned, zero), jnp.where(lane < BLK, zero, turned)], axis=0
        ).astype(BF16)
        term = lax.dot_general(
            weights, left, (((1,), (1,)), ((), ())), preferred_element_type=F32
        )
        for n in range(4):
            b = kept[(i * nb + g * group + pairs * 2) * 2 + n]
            at_rows = pl.ds(pl.multiple_of(b * BLK, BLK), BLK)
            total[at_rows, :] += term[n * BLK:(n + 1) * BLK]

    @pl.when((i == pl.num_programs(0) - 1) & (g == pl.num_programs(1) - 1))
    def _():
        def turn(t, _):
            cols = pl.ds(pl.multiple_of(t * LANES, LANES), LANES)
            out[:, cols] = total[cols, :].T.astype(BF16)
            return 0

        lax.fori_loop(0, out.shape[1] // LANES, turn, 0, unroll=2)


def toward_second(kept, first, amp, group=8):
    ni, rows, width = first.shape
    nb = width // BLK
    groups = nb // group
    return pl.pallas_call(
        functools.partial(toward_second_kernel, group, nb),
        out_shape=jax.ShapeDtypeStruct((rows, width), BF16),
        grid_spec=pltpu.PrefetchScalarGridSpec(
            num_scalar_prefetch=1,
            grid=(ni, groups),
            in_specs=[
                pl.BlockSpec((1, rows, group * BLK), lambda i, g, kept: (i, 0, g)),
                pl.BlockSpec((group, BLK, LANES), lambda i, g, kept: (i * groups + g, 0, 0)),
            ],
            out_specs=pl.BlockSpec((rows, width), lambda i, g, kept: (0, 0)),
            scratch_shapes=[pltpu.VMEM((width, rows), F32)],
        ),
        compiler_params=pltpu.CompilerParams(vmem_limit_bytes=VMEM_LIMIT),
        name="toward_second",
    )(kept, first, amp)


def shards(first_factors, second_factors, first_energy, second_energy, virtual_energy, kept_blocks):
    naux, nz = lax.axis_size("aux"), lax.axis_size("occ") // 2
    a, z, c, p = place()
    rows, nj, width = second_factors.shape
    frows, ni, _ = first_factors.shape
    nb = width // BLK
    entries = ni * nb

    order = [
        (aa * 2 * nz + zz * 2 + cc, zz * 2 * nz + aa * 2 + cc)
        for aa in range(naux) for zz in range(nz) for cc in range(2)
    ]
    kept_here = kept_blocks[:, 0].reshape(entries * 2)
    kept_mine = lax.ppermute(kept_here, ("aux", "occ"), order)
    energy_mine = lax.ppermute(second_energy, ("aux", "occ"), order)
    swap = [(o, o // 2 * 2 + 1 - o % 2) for o in range(2 * nz)]
    kept_twin = lax.ppermute(kept_mine, "occ", swap)
    kept = jnp.concatenate([kept_mine, kept_twin])
    tiles = kept // 2
    in_place = jnp.stack([kept[0::2] % 2 == 0, kept[1::2] % 2 == 1], axis=1)
    straight = jnp.repeat(in_place.astype(F32), BLK, axis=1)

    size = entries // nz
    energy_blocks = virtual_energy.reshape(nb, BLK)
    picked = lax.dynamic_slice_in_dim(kept_mine, z * size * 2, size * 2, 0)
    entry = z * size + jnp.arange(size)
    left = jnp.take(energy_blocks, entry % nb, axis=0)
    right = jnp.take(energy_blocks, picked, axis=0).reshape(size, 2 * BLK)
    low = jnp.take(first_energy, entry // nb)
    divisor = left[:, :, None] + right[:, None, :] - low[:, None, None] - energy_mine[0]

    second = jnp.transpose(second_factors, (1, 0, 2)).reshape(naux, 2, 2, rows, width)
    first = jnp.transpose(first_factors, (1, 0, 2))
    sec, firstz, firsta = spread(second, first, naux, nz)
    sec = sec.reshape(2, naux * 2 * rows, width)
    firstz = firstz.reshape(ni, naux * frows, width)
    firsta = firsta.reshape(ni, nz * 2 * frows, width)

    amp1, mine = amplitudes(tiles, sec, firstz, straight, divisor, naux, nz)
    first_density, amp2 = first_density_of(tiles, sec, amp1, mine, straight, naux, nz)
    amp2 = amp2.reshape(entries, BLK, LANES)
    second_density = toward_second(kept_here, firsta, amp2)
    return (
        first_density.reshape(nz * 2 * frows, 1, width // (nz * 2)),
        second_density.reshape(nz * 2 * frows, 1, width),
    )


def solution(mesh):
    placed = (
        P(("aux", "occ"), None, None),
        P(("aux", "occ", "pair"), None, None),
        P(),
        P(("occ", "pair")),
        P(),
        P(None, ("occ", "pair"), None, None),
    )
    return jax.shard_map(
        shards,
        mesh=mesh,
        in_specs=placed,
        out_specs=(P("aux", "pair", "occ"), P("aux", ("occ", "pair"), None)),
        check_vma=False,
    )
```

```python
import functools

import jax
import jax.numpy as jnp
from jax import lax
from jax.experimental import pallas as pl
from jax.experimental.pallas import tpu as pltpu
from jax.sharding import PartitionSpec as P

MESH = pl.DeviceIdType.MESH
F32 = jnp.float32
BF16 = jnp.bfloat16
BLK = 64
LANES = 128
NX = 4
ORDER = (
    (1, 0), (0, 1), (3, 0), (0, 3), (1, 1), (3, 3), (1, 3), (3, 1),
    (2, 0), (0, 2), (2, 1), (1, 2), (2, 3), (3, 2), (2, 2),
)
LINE = ((1, 0), (3, 0), (0, 1), (2, 0), (1, 1), (3, 1), (2, 1))
VMEM_LIMIT = 52 * 1024 * 1024


def place():
    aux, occ, pair = lax.axis_index("aux"), lax.axis_index("occ"), lax.axis_index("pair")
    return aux, occ // 2, occ % 2, pair


def device(aux, z, core, pair):
    return {"aux": aux, "occ": z * 2 + core, "pair": pair}


def push(src, dst, send, recv, to):
    copy = pltpu.make_async_remote_copy(
        src_ref=src, dst_ref=dst, send_sem=send, recv_sem=recv, device_id=to, device_id_type=MESH
    )
    copy.start()
    return copy


def landed(ref, send, recv, to):
    pltpu.make_async_remote_copy(
        src_ref=ref, dst_ref=ref, send_sem=send, recv_sem=recv, device_id=to, device_id_type=MESH
    ).wait_recv()


def greet(peers):
    barrier = pltpu.get_barrier_semaphore()
    for peer in peers:
        pl.semaphore_signal(barrier, inc=1, device_id=peer, device_id_type=MESH)
    pl.semaphore_wait(barrier, len(peers))


def plane_peers(a, z, c, p, naux):
    return [
        device((a + da) % naux, z, c, (p + dp) % 2)
        for da in range(naux)
        for dp in range(2)
        if (da, dp) != (0, 0)
    ]


class Ring:
    def __init__(self, block, half, z, nz, c, me, sems):
        self.block, self.half, self.z, self.nz, self.c = block, half, z, nz, c
        self.me = me
        self.up_send, self.up_recv, self.dn_send, self.dn_recv, self.co_send, self.co_recv = sems
        self.up, self.dn, self.co = me(1, 0), me(-1, 0), me(0, 1)
        self.far = nz // 2
        self.sent = []

    def piece(self, way, step, core):
        origin = (self.z - way * (step + 1) + self.nz) % self.nz
        if step + 1 == self.far:
            return self.half(origin, core, 0 if way > 0 else 1)
        return self.block(origin, core)

    def start(self, source, source_halves):
        mine = self.block(self.z, self.c)
        if self.far == 1:
            raise ValueError("short ring")
        self.sent.append(push(source, mine, self.up_send.at[0], self.up_recv.at[0], self.up))
        self.sent.append(push(source, mine, self.dn_send.at[0], self.dn_recv.at[0], self.dn))
        self.sent.append(push(source, mine, self.co_send.at[0], self.co_recv.at[0], self.co))

    def step(self, step):
        for way, send, recv, to in (
            (1, self.up_send, self.up_recv, self.up),
            (-1, self.dn_send, self.dn_recv, self.dn),
        ):
            got = self.piece(way, step, self.c)
            landed(got, send.at[step], recv.at[step], to)
            if step + 1 < self.far:
                onward = got
                if step + 2 == self.far:
                    origin = (self.z - way * (step + 1) + self.nz) % self.nz
                    onward = self.half(origin, self.c, 0 if way > 0 else 1)
                self.sent.append(push(onward, onward, send.at[step + 1], recv.at[step + 1], to))
            k = 1 + 2 * step + (0 if way > 0 else 1)
            self.sent.append(push(got, got, self.co_send.at[k], self.co_recv.at[k], self.co))

    def finish(self):
        other = 1 - self.c
        landed(self.block(self.z, other), self.co_send.at[0], self.co_recv.at[0], self.co)
        for step in range(self.far):
            for way in (1, -1):
                k = 1 + 2 * step + (0 if way > 0 else 1)
                landed(self.piece(way, step, other), self.co_send.at[k], self.co_recv.at[k], self.co)
        for copy in self.sent:
            copy.wait_send()


def ring_sems(nz):
    far = nz // 2
    return [pltpu.SemaphoreType.DMA((far,))] * 4 + [pltpu.SemaphoreType.DMA((1 + 2 * far,))] * 2


def spread_kernel(
    naux, nz, second, first, sec, firstz, firsta, a_send, a_recv, b_send, b_recv, loc, *sems
):
    a, z, c, p = place()
    x, yh = a // 2, a % 2

    def me(dz, dc):
        return device(a, (z + dz + nz) % nz, (c + dc) % 2, p)

    in_plane = plane_peers(a, z, c, p, naux)
    greet(in_plane + [me(1, 0), me(-1, 0), me(0, 1)])

    locals_ = [
        pltpu.make_async_copy(first, firstz.at[:, a], loc.at[0]),
        pltpu.make_async_copy(first, firsta.at[:, z * 2 + c], loc.at[1]),
        pltpu.make_async_copy(second.at[a, :, p], sec.at[:, a * 2 + p], loc.at[2]),
    ]
    sent = []
    right = device((x + 1) % NX * 2 + yh, z, c, p)
    left = device((x + NX - 1) % NX * 2 + yh, z, c, p)
    across = device(x * 2 + (1 - yh), z, c, 1 - p)
    beside = device(a, z, c, 1 - p)
    al = (x + NX - 1) % NX * 2 + yh
    ar = (x + 1) % NX * 2 + yh
    af = (x + 2) % NX * 2 + yh
    sent.append(push(first, firstz.at[:, a], b_send.at[0], b_recv.at[0], right))
    sent.append(push(first, firstz.at[:, a], b_send.at[1], b_recv.at[1], left))
    sent.append(push(first.at[p], firstz.at[p, a], b_send.at[4], b_recv.at[4], across))
    ring = Ring(
        lambda zz, cc: firsta.at[:, zz * 2 + cc],
        lambda zz, cc, h: firsta.at[h, zz * 2 + cc],
        z, nz, c, me, sems,
    )
    ring.start(first, None)
    y = yh * 2 + p
    batches = [4, 2, 2, 2, 2, 2, 1]

    def plane(dx, dy):
        ty = (y + dy) % 4
        return (x + dx) % NX * 2 + ty // 2, ty % 2

    def send_some():
        for _ in range(batches.pop(0) if batches else 0):
            n = len(second_sent)
            ta, tp = plane(*ORDER[n])
            second_sent.append(
                push(second.at[ta, :, tp], sec.at[:, a * 2 + p], a_send.at[n], a_recv.at[n],
                     device(ta, z, c, tp))
            )

    second_sent = []
    send_some()
    for copy in locals_:
        copy.start()

    landed(firstz.at[:, al], b_send.at[0], b_recv.at[0], left)
    sent.append(push(firstz.at[0, al], firstz.at[0, al], b_send.at[2], b_recv.at[2], right))
    sent.append(push(firstz.at[p, al], firstz.at[p, al], b_send.at[5], b_recv.at[5], across))
    send_some()
    landed(firstz.at[:, ar], b_send.at[1], b_recv.at[1], right)
    sent.append(push(firstz.at[1, ar], firstz.at[1, ar], b_send.at[3], b_recv.at[3], left))
    sent.append(push(firstz.at[p, ar], firstz.at[p, ar], b_send.at[6], b_recv.at[6], across))
    send_some()
    ring.step(0)
    send_some()

    def relay(k, slot):
        got = firstz.at[1 - p, slot // 2 * 2 + (1 - yh)]
        landed(got, b_send.at[4 + k], b_recv.at[4 + k], across)
        sent.append(push(got, got, b_send.at[8 + k], b_recv.at[8 + k], beside))

    relay(0, a)
    send_some()
    landed(firstz.at[0, af], b_send.at[2], b_recv.at[2], left)
    landed(firstz.at[1, af], b_send.at[3], b_recv.at[3], right)
    sent.append(push(firstz.at[p, af], firstz.at[p, af], b_send.at[7], b_recv.at[7], across))
    send_some()
    ring.step(1)
    send_some()
    relay(1, al)
    relay(2, ar)
    ring.step(2)
    relay(3, af)
    ring.step(3)
    for k, slot in enumerate((a, al, ar, af)):
        got = firstz.at[p, slot // 2 * 2 + (1 - yh)]
        landed(got, b_send.at[8 + k], b_recv.at[8 + k], beside)
    ring.finish()
    for n, (dx, dy) in enumerate(ORDER):
        fa, fp = plane(NX - dx, 4 - dy)
        landed(sec.at[:, fa * 2 + fp], a_send.at[n], a_recv.at[n], device(fa, z, c, fp))
    for copy in second_sent:
        copy.wait_send()
    for copy in sent:
        copy.wait_send()
    for copy in locals_:
        copy.wait()


def spread(second, first, naux, nz):
    _, _, _, rows, width = second.shape
    ni, frows, _ = first.shape
    return pl.pallas_call(
        functools.partial(spread_kernel, naux, nz),
        out_shape=[
            jax.ShapeDtypeStruct((2, naux * 2, rows, width), BF16),
            jax.ShapeDtypeStruct((ni, naux, frows, width), BF16),
            jax.ShapeDtypeStruct((ni, nz * 2, frows, width), BF16),
        ],
        in_specs=[pl.BlockSpec(memory_space=pl.ANY)] * 2,
        out_specs=[pl.BlockSpec(memory_space=pl.ANY)] * 3,
        scratch_shapes=[
            pltpu.SemaphoreType.DMA((naux * 2 - 1,)),
            pltpu.SemaphoreType.DMA((naux * 2 - 1,)),
            pltpu.SemaphoreType.DMA((12,)),
            pltpu.SemaphoreType.DMA((12,)),
            pltpu.SemaphoreType.DMA((3,)),
            *ring_sems(nz),
        ],
        compiler_params=pltpu.CompilerParams(
            collective_id=1, has_side_effects=True, vmem_limit_bytes=VMEM_LIMIT
        ),
        name="spread",
    )(second, first)


def load_tiles(sec_hbm, sec, sem):
    return [
        pltpu.make_async_copy(sec_hbm.at[:, :, pl.ds(t * LANES, LANES)], sec.at[:, t], sem.at[t])
        for t in range(sec.shape[1])
    ]


def spread_masked(amp, straight):
    lane = lax.broadcasted_iota(jnp.int32, (BLK, LANES), 1)
    zero = jnp.zeros_like(amp)
    stay = jnp.where(straight, amp, zero)
    move = pltpu.roll(jnp.where(straight, zero, amp), BLK, 1)
    return jnp.where(lane < BLK, stay, move), jnp.where(lane < BLK, move, stay)


def amplitude_kernel(
    naux, nz, nb, tiles, sec_hbm, first_hbm, straight, divisor, amp, mine,
    sec, first, own, other, twin, outgoing, got, shard,
    d_send, d_recv, r_send, r_recv, t_send, t_recv, s_load, loc, *sems
):
    a, z, c, p = place()
    size = divisor.shape[0]
    loads = [pltpu.make_async_copy(first_hbm, first, loc.at[0]), *load_tiles(sec_hbm, sec, s_load)]
    for load in loads:
        load.start()
    far, half = nz // 2, size // 2

    def me(dz, dc):
        return device(a, (z + dz) % nz, (c + dc) % 2, p)

    sibling = me(0, 1)
    line = [device((a + da) % naux, z, c, p) for da in range(1, naux)]
    greet([sibling, me(1, 0), me(nz - 1, 0)] + line)
    for load in loads:
        load.wait()
    lane = lax.broadcasted_iota(jnp.int32, (BLK, LANES), 1)

    def rows(t):
        return pl.ds(t * size, size)

    sent = []

    def compute(dz):
        t = (z + dz) % nz
        i, start = t * size // nb, t * size % nb

        def two(k, _):
            tile = pl.ds(pl.multiple_of((start // 2 + k) * LANES, LANES), LANES)
            left = first[i, :, tile].T
            for side, out in ((0, own), (1, other)):
                which = c if side == 0 else 1 - c
                for e in range(2):
                    at = (side * 2 + i) * nb + start + k * 2 + e
                    right = jnp.concatenate(
                        [sec[which, tiles[at * 2]], sec[which, tiles[at * 2 + 1]]], axis=1
                    )
                    prod = lax.dot_general(
                        left[e * BLK:(e + 1) * BLK], right, (((1,), (0,)), ((), ())),
                        preferred_element_type=F32,
                    )
                    u0, u1 = prod[:, :LANES], prod[:, LANES:]
                    stay = jnp.where(lane < BLK, u0, u1)
                    move = pltpu.roll(jnp.where(lane < BLK, u1, u0), BLK, 1)
                    chosen = jnp.where(straight[pl.ds(at, 1), :] > 0.5, stay, move)
                    out[t * size + k * 2 + e] = chosen.astype(out.dtype)
            return 0

        lax.fori_loop(0, size // 2, two, 0)
        sent.append(
            push(other.at[rows(t)], twin.at[rows(t)], d_send.at[dz], d_recv.at[dz], sibling)
        )

    ways = ((1, 0, me(1, 0)), (-1, 1, me(nz - 1, 0)))

    def reduce_step(step, way, w, to):
        dz = way * (far - step) % nz
        t = (z + dz) % nz
        if step or w == 0:
            landed(twin.at[rows(t)], d_send.at[dz], d_recv.at[dz], sibling)

        def add(k, _):
            n = t * size + k
            total = own[n] + twin[n].astype(F32)
            outgoing[w, step, k] = total.astype(BF16)
            return 0

        def add_got(k, _):
            n = t * size + k
            total = own[n] + twin[n].astype(F32) + got[w, step - 1, k].astype(F32)
            outgoing[w, step, k] = total.astype(BF16)
            return 0

        for h in (1 - w, w):
            if step == 0 and h != w:
                continue
            span = pl.ds(h * half, half)
            if step > 1 or (step == 1 and h == w):
                landed(got.at[w, step - 1, span], r_send.at[w, step - 1, h],
                       r_recv.at[w, step - 1, h], to)
                lax.fori_loop(h * half, h * half + half, add_got, 0, unroll=4)
            else:
                lax.fori_loop(h * half, h * half + half, add, 0, unroll=4)
            sent.append(
                push(outgoing.at[w, step, span], got.at[w, step, span],
                     r_send.at[w, step, h], r_recv.at[w, step, h], to)
            )

    compute(far)
    compute(far - 1)
    reduce_step(0, *ways[0])
    reduce_step(0, *ways[1])
    for step in range(1, far):
        compute(nz - far + step)
        reduce_step(step, *ways[0])
        compute(far - 1 - step)
        reduce_step(step, *ways[1])

    landed(twin.at[rows(z)], d_send.at[0], d_recv.at[0], sibling)
    for way, w, to in ways:
        for h in range(2):
            landed(got.at[w, far - 1, pl.ds(h * half, half)], r_send.at[w, far - 1, h],
                   r_recv.at[w, far - 1, h], to)

    def reduce(k, _):
        n = z * size + k
        total = own[n] + twin[n].astype(F32)
        total = total + got[0, far - 1, k].astype(F32) + got[1, far - 1, k].astype(F32)
        shard[k] = (total / divisor[k]).astype(BF16)
        return 0

    lax.fori_loop(0, size, reduce, 0, unroll=2)

    ring = Ring(
        lambda zz, cc: amp.at[cc, pl.ds(zz * size, size)],
        lambda zz, cc, h: amp.at[cc, pl.ds(zz * size + h * half, half)],
        z, nz, c, lambda dz, dc: me((dz + nz) % nz, dc), sems,
    )
    ring.start(shard, None)
    here = pltpu.make_async_copy(shard, amp.at[c, rows(z)], loc.at[1])
    here.start()

    keep = pltpu.make_async_copy(shard, mine, loc.at[2])

    @pl.when(a == z)
    def _():
        keep.start()

    def hand_out(n, start):
        s = (z + n) % nz
        copy = pltpu.make_async_remote_copy(
            src_ref=amp.at[c, rows(s)], dst_ref=mine, send_sem=t_send.at[n - 1],
            recv_sem=t_recv.at[0], device_id=device(s, z, c, p), device_id_type=MESH,
        )
        if start:
            copy.start()
        else:
            copy.wait_send()

    for step in range(far):
        ring.step(step)

        @pl.when(a == z)
        def _():
            for n in sorted({step + 1, nz - 1 - step}):
                hand_out(n, True)

    ring.finish()

    @pl.when(a == z)
    def _():
        keep.wait()
        for n in range(1, nz):
            hand_out(n, False)

    @pl.when(a != z)
    def _():
        landed(mine, t_send.at[0], t_recv.at[0], device(z, z, c, p))

    here.wait()
    for copy in sent:
        copy.wait_send()


def amplitudes(tiles, sec, first, straight, divisor, naux, nz):
    ni, _, width = first.shape
    nb = width // BLK
    entries = ni * nb
    size = divisor.shape[0]
    block = (BLK, LANES)
    dma = pltpu.SemaphoreType.DMA
    vmem = pl.BlockSpec(memory_space=pltpu.VMEM)
    hbm = pl.BlockSpec(memory_space=pl.ANY)
    return pl.pallas_call(
        functools.partial(amplitude_kernel, naux, nz, nb),
        out_shape=[
            jax.ShapeDtypeStruct((2, entries, *block), BF16),
            jax.ShapeDtypeStruct((size, *block), BF16),
        ],
        in_specs=[pl.BlockSpec(memory_space=pltpu.SMEM), hbm, hbm, vmem, vmem],
        out_specs=[hbm, hbm],
        scratch_shapes=[
            pltpu.VMEM((2, width // LANES, sec.shape[1], LANES), BF16),
            pltpu.VMEM(first.shape, BF16),
            pltpu.VMEM((entries, *block), F32),
            pltpu.VMEM((entries, *block), BF16),
            pltpu.VMEM((entries, *block), BF16),
            pltpu.VMEM((2, nz // 2, size, *block), BF16),
            pltpu.VMEM((2, nz // 2, size, *block), BF16),
            pltpu.VMEM((size, *block), BF16),
            dma((nz,)), dma((nz,)), dma((2, nz // 2, 2)), dma((2, nz // 2, 2)),
            dma((nz - 1,)), dma((1,)), dma((width // LANES,)), dma((3,)),
            *ring_sems(nz),
        ],
        compiler_params=pltpu.CompilerParams(
            collective_id=2, has_side_effects=True, vmem_limit_bytes=VMEM_LIMIT
        ),
        name="amplitudes",
    )(tiles, sec, first, straight, divisor)


class Sum:
    def __init__(self, me, up, dn, s0, r0, s1, r1):
        self.me, self.up, self.dn = me, up, dn
        self.s0, self.r0, self.s1, self.r1 = s0, r0, s1, r1

    def first(self, part, into):
        far = (self.me + 2) % 4
        return [
            push(part(far, w), into(w), self.s0.at[w], self.r0.at[w], to)
            for w, to in ((0, self.up), (1, self.dn))
        ]

    def first_landed(self, into):
        for w, to in ((0, self.dn), (1, self.up)):
            landed(into(w), self.s0.at[w], self.r0.at[w], to)

    def second(self, source, into):
        return [
            push(source(w), into(w), self.s1.at[w], self.r1.at[w], to)
            for w, to in ((0, self.up), (1, self.dn))
        ]

    def second_landed(self, into):
        for w, to in ((0, self.dn), (1, self.up)):
            landed(into(w), self.s1.at[w], self.r1.at[w], to)


def first_density_kernel(
    naux, nz, nb, tiles, sec_hbm, amp_hbm, mine, straight, out, amps,
    sec, amp, part, got_a, give_b, got_b, total, give_c, got_c, give_d, got_d, done,
    p1s, p1r, p2s, p2r, z_send, z_recv, x_send, x_recv, s_load, loc
):
    a, z, c, p = place()
    loads = [pltpu.make_async_copy(amp_hbm, amp, loc.at[0]), *load_tiles(sec_hbm, sec, s_load)]
    for load in loads:
        load.start()
    x, y = a // 2, a % 2 * 2 + p
    frows, width = part.shape[3], part.shape[4]
    group = width // BLK
    chunk_half = width // 2

    def me(dz, dc):
        return device(a, (z + dz) % nz, (c + dc) % 2, p)

    def at_y(ty):
        return device(x * 2 + ty // 2, z, c, ty % 2)

    column = [(dz, dc) for dz in range(nz) for dc in range(2) if (dz, dc) != (0, 0)]
    right, left = device((a + 2) % naux, z, c, p), device((a + naux - 2) % naux, z, c, p)
    above, below = at_y((y + 1) % 4), at_y((y + 3) % 4)
    yh = a % 2
    line = [device((x + dx) % NX * 2 + (yh + dy) % 2, z, c, p) for dx, dy in LINE]
    greet(line + [above, below] + [me(dz, dc) for dz, dc in column])
    keep = pltpu.make_async_copy(mine, amps.at[a], loc.at[2])
    keep.start()
    for load in loads:
        load.wait()
    sent = []

    def pass_on(n):
        sent.append(push(mine, amps.at[a], x_send.at[n], x_recv.at[n], line[n]))

    def compute(k):
        chunk = (z + 1 + k) % nz

        def orbital(i, _):
            for m in range(group // 2):
                halves = []
                for e in range(2):
                    entry = chunk * group + m * 2 + e
                    rights, weights = [], []
                    for side in range(2):
                        core = c if side == 0 else 1 - c
                        at = (side * 2 + i) * nb + entry
                        rights += [sec[core, tiles[at * 2]], sec[core, tiles[at * 2 + 1]]]
                        weights += spread_masked(
                            amp[core, i * nb + entry].astype(F32), straight[pl.ds(at, 1), :] > 0.5
                        )
                    halves.append(
                        lax.dot_general(
                            jnp.concatenate(rights, axis=1),
                            jnp.concatenate(weights, axis=1).astype(BF16),
                            (((1,), (1,)), ((), ())),
                            preferred_element_type=F32,
                        )
                    )
                both = jnp.concatenate(halves, axis=1).astype(BF16)
                both = both.reshape(4, 2, frows, LANES)
                cols = slice(m * LANES, (m + 1) * LANES)
                for xx in range(4):
                    for yy in range(2):
                        u, v = (xx, yy * 2 + i) if k % 2 == 0 else (yy * 2 + i, xx)
                        part[k, u, v, :, cols] = both[xx, yy]
            return 0

        lax.fori_loop(0, 2, orbital, 0)

    def rings(k):
        over_x = (x, right, left)
        over_y = (y, above, below)
        one, two = (over_x, over_y) if k % 2 == 0 else (over_y, over_x)
        return (
            Sum(*one, p1s.at[k, 0], p1r.at[k, 0], p1s.at[k, 1], p1r.at[k, 1]),
            Sum(*two, p2s.at[k, 0], p2r.at[k, 0], p2s.at[k, 1], p2r.at[k, 1]),
        )

    def stage_b(k):
        one, _ = rings(k)
        sent.extend(
            one.first(
                lambda far, w: part.at[k, far, pl.ds(2 * w, 2)], lambda w: got_a.at[k, w]
            )
        )

    def stage_c(k):
        one, _ = rings(k)
        one.first_landed(lambda w: got_a.at[k, w])
        for w, step in ((0, 1), (1, 3)):
            u = (one.me + step) % 4
            for v in range(4):
                if v // 2 == w:
                    both = part[k, u, v].astype(F32) + got_a[k, w, v % 2].astype(F32)
                    give_b[k, w, v] = both.astype(BF16)
                else:
                    give_b[k, w, v] = part[k, u, v]
        sent.extend(one.second(lambda w: give_b.at[k, w], lambda w: got_b.at[k, w]))

    def stage_d(k):
        one, two = rings(k)
        one.second_landed(lambda w: got_b.at[k, w])
        for v in range(4):
            total[k, v] = (
                part[k, one.me, v].astype(F32)
                + got_b[k, 0, v].astype(F32) + got_b[k, 1, v].astype(F32)
            )
        far = (two.me + 2) % 4
        for w in range(2):
            give_c[k, w] = total[k, far, :, w * chunk_half:(w + 1) * chunk_half].astype(BF16)
        sent.extend(two.first(lambda far, w: give_c.at[k, w], lambda w: got_c.at[k, w]))

    def stage_e(k):
        _, two = rings(k)
        two.first_landed(lambda w: got_c.at[k, w])
        for w, step in ((0, 1), (1, 3)):
            v = (two.me + step) % 4
            for h in range(2):
                cols = slice(h * chunk_half, (h + 1) * chunk_half)
                mine = total[k, v, :, cols]
                if h == w:
                    mine = mine + got_c[k, w].astype(F32)
                give_d[k, w, :, cols] = mine.astype(BF16)
        sent.extend(two.second(lambda w: give_d.at[k, w], lambda w: got_d.at[k, w]))

    def stage_f(k):
        _, two = rings(k)
        two.second_landed(lambda w: got_d.at[k, w])
        final = total[k, two.me] + got_d[k, 0].astype(F32) + got_d[k, 1].astype(F32)
        done[k] = final.astype(BF16)
        dz = (k + 1) % nz
        for dc in range(2):
            cc = (c + dc) % 2
            source = done.at[k, :, pl.ds(pl.multiple_of(cc * chunk_half, chunk_half), chunk_half)]
            if (dz, dc) == (0, 0):
                pltpu.make_async_copy(source, out.at[z * 2 + c], loc.at[1]).start()
            else:
                n = dz * 2 + dc
                sent.append(
                    push(source, out.at[z * 2 + c], z_send.at[n], z_recv.at[n], me(dz, dc))
                )

    stages = ((stage_b, 0), (stage_c, 2), (stage_d, 5), (stage_e, 7), (stage_f, 9))
    waiting = list(range(len(line)))
    for k in range(nz + stages[-1][1]):
        if k < nz:
            compute(k)
        for stage, lag in stages:
            if 0 <= k - lag < nz:
                stage(k - lag)
        if waiting:
            pass_on(waiting.pop(0))

    for dz, dc in column:
        fz, fc = (z - dz + nz) % nz, (c + dc) % 2
        n = dz * 2 + dc
        landed(out.at[fz * 2 + fc], z_send.at[n], z_recv.at[n], device(a, fz, fc, p))
    pltpu.make_async_copy(
        done.at[nz - 1, :, pl.ds(pl.multiple_of(c * chunk_half, chunk_half), chunk_half)],
        out.at[z * 2 + c], loc.at[1],
    ).wait()
    keep.wait()
    for n, (dx, dy) in enumerate(LINE):
        fa = (x - dx + NX) % NX * 2 + (yh + dy) % 2
        landed(amps.at[fa], x_send.at[n], x_recv.at[n], device(fa, z, c, p))
    for copy in sent:
        copy.wait_send()


def first_density_of(tiles, sec, amp, mine, straight, naux, nz):
    _, rows, width = sec.shape
    nb = width // BLK
    frows, chunk = rows // naux, width // nz
    dma = pltpu.SemaphoreType.DMA
    hbm = pl.BlockSpec(memory_space=pl.ANY)
    return pl.pallas_call(
        functools.partial(first_density_kernel, naux, nz, nb),
        out_shape=[
            jax.ShapeDtypeStruct((nz * 2, frows, chunk // 2), BF16),
            jax.ShapeDtypeStruct((naux, *mine.shape), BF16),
        ],
        in_specs=[
            pl.BlockSpec(memory_space=pltpu.SMEM), hbm, hbm, hbm,
            pl.BlockSpec(memory_space=pltpu.VMEM),
        ],
        out_specs=[hbm, hbm],
        scratch_shapes=[
            pltpu.VMEM((2, width // LANES, rows, LANES), BF16),
            pltpu.VMEM(amp.shape, BF16),
            pltpu.VMEM((nz, 4, 4, frows, chunk), BF16),
            pltpu.VMEM((nz, 2, 2, frows, chunk), BF16),
            pltpu.VMEM((nz, 2, 4, frows, chunk), BF16),
            pltpu.VMEM((nz, 2, 4, frows, chunk), BF16),
            pltpu.VMEM((nz, 4, frows, chunk), F32),
            pltpu.VMEM((nz, 2, frows, chunk // 2), BF16),
            pltpu.VMEM((nz, 2, frows, chunk // 2), BF16),
            pltpu.VMEM((nz, 2, frows, chunk), BF16),
            pltpu.VMEM((nz, 2, frows, chunk), BF16),
            pltpu.VMEM((nz, frows, chunk), BF16),
            dma((nz, 2, 2)), dma((nz, 2, 2)), dma((nz, 2, 2)), dma((nz, 2, 2)),
            dma((nz * 2,)), dma((nz * 2,)), dma((naux - 1,)), dma((naux - 1,)),
            dma((width // LANES,)), dma((3,)),
        ],
        compiler_params=pltpu.CompilerParams(
            collective_id=3, has_side_effects=True, vmem_limit_bytes=VMEM_LIMIT
        ),
        name="first_density",
    )(tiles, sec, amp, mine, straight)


def toward_second_kernel(group, nb, kept, first, amp, out, total):
    i, g = pl.program_id(0), pl.program_id(1)

    @pl.when((i == 0) & (g == 0))
    def _():
        total[...] = jnp.zeros_like(total)

    lane = lax.broadcasted_iota(jnp.int32, (LANES, LANES), 1)
    for pairs in range(group // 2):
        left = first[0, :, pairs * LANES:(pairs + 1) * LANES]
        turned = jnp.concatenate(
            [amp[pairs * 2].astype(F32), amp[pairs * 2 + 1].astype(F32)], axis=0
        ).T
        zero = jnp.zeros_like(turned)
        weights = jnp.concatenate(
            [jnp.where(lane < BLK, turned, zero), jnp.where(lane < BLK, zero, turned)], axis=0
        ).astype(BF16)
        term = lax.dot_general(
            weights, left, (((1,), (1,)), ((), ())), preferred_element_type=F32
        )
        for n in range(4):
            b = kept[(i * nb + g * group + pairs * 2) * 2 + n]
            at_rows = pl.ds(pl.multiple_of(b * BLK, BLK), BLK)
            total[at_rows, :] += term[n * BLK:(n + 1) * BLK]

    @pl.when((i == pl.num_programs(0) - 1) & (g == pl.num_programs(1) - 1))
    def _():
        def turn(t, _):
            cols = pl.ds(pl.multiple_of(t * LANES, LANES), LANES)
            out[:, cols] = total[cols, :].T.astype(BF16)
            return 0

        lax.fori_loop(0, out.shape[1] // LANES, turn, 0, unroll=2)


def toward_second(kept, first, amp, group=16):
    ni, rows, width = first.shape
    nb = width // BLK
    groups = nb // group
    return pl.pallas_call(
        functools.partial(toward_second_kernel, group, nb),
        out_shape=jax.ShapeDtypeStruct((rows, width), BF16),
        grid_spec=pltpu.PrefetchScalarGridSpec(
            num_scalar_prefetch=1,
            grid=(ni, groups),
            in_specs=[
                pl.BlockSpec((1, rows, group * BLK), lambda i, g, kept: (i, 0, g)),
                pl.BlockSpec((group, BLK, LANES), lambda i, g, kept: (i * groups + g, 0, 0)),
            ],
            out_specs=pl.BlockSpec((rows, width), lambda i, g, kept: (0, 0)),
            scratch_shapes=[pltpu.VMEM((width, rows), F32)],
        ),
        compiler_params=pltpu.CompilerParams(vmem_limit_bytes=VMEM_LIMIT),
        name="toward_second",
    )(kept, first, amp)


def shards(first_factors, second_factors, first_energy, second_energy, virtual_energy, kept_blocks):
    naux, nz = lax.axis_size("aux"), lax.axis_size("occ") // 2
    a, z, c, p = place()
    rows, nj, width = second_factors.shape
    frows, ni, _ = first_factors.shape
    nb = width // BLK
    entries = ni * nb

    order = [
        (aa * 2 * nz + zz * 2 + cc, zz * 2 * nz + aa * 2 + cc)
        for aa in range(naux) for zz in range(nz) for cc in range(2)
    ]
    kept_here = kept_blocks[:, 0].reshape(entries * 2)
    kept_mine = lax.ppermute(kept_here, ("aux", "occ"), order)
    energy_mine = lax.ppermute(second_energy, ("aux", "occ"), order)
    crossed = [(source, target + 1 - 2 * (target % 2)) for source, target in order]
    kept_twin = lax.ppermute(kept_here, ("aux", "occ"), crossed)
    kept = jnp.concatenate([kept_mine, kept_twin])
    tiles = kept // 2
    in_place = jnp.stack([kept[0::2] % 2 == 0, kept[1::2] % 2 == 1], axis=1)
    straight = jnp.repeat(in_place.astype(F32), BLK, axis=1)

    size = entries // nz
    energy_blocks = virtual_energy.reshape(nb, BLK)
    picked = lax.dynamic_slice_in_dim(kept_mine, z * size * 2, size * 2, 0)
    entry = z * size + jnp.arange(size)
    left = jnp.take(energy_blocks, entry % nb, axis=0)
    right = jnp.take(energy_blocks, picked, axis=0).reshape(size, 2 * BLK)
    low = jnp.take(first_energy, entry // nb)
    divisor = left[:, :, None] + right[:, None, :] - low[:, None, None] - energy_mine[0]

    second = jnp.transpose(second_factors, (1, 0, 2)).reshape(naux, 2, 2, rows, width)
    first = jnp.transpose(first_factors, (1, 0, 2))
    sec, firstz, firsta = spread(second, first, naux, nz)
    sec = sec.reshape(2, naux * 2 * rows, width)
    firstz = firstz.reshape(ni, naux * frows, width)
    firsta = firsta.reshape(ni, nz * 2 * frows, width)

    amp1, mine = amplitudes(tiles, sec, firstz, straight, divisor, naux, nz)
    first_density, amp2 = first_density_of(tiles, sec, amp1, mine, straight, naux, nz)
    amp2 = amp2.reshape(entries, BLK, LANES)
    second_density = toward_second(kept_here, firsta, amp2)
    return (
        first_density.reshape(nz * 2 * frows, 1, width // (nz * 2)),
        second_density.reshape(nz * 2 * frows, 1, width),
    )


def solution(mesh):
    placed = (
        P(("aux", "occ"), None, None),
        P(("aux", "occ", "pair"), None, None),
        P(),
        P(("occ", "pair")),
        P(),
        P(None, ("occ", "pair"), None, None),
    )
    return jax.shard_map(
        shards,
        mesh=mesh,
        in_specs=placed,
        out_specs=(P("aux", "pair", "occ"), P("aux", ("occ", "pair"), None)),
        check_vma=False,
    )
```
